32 devices in a mesh: ctx: 8 (over z, x), head: 4 (over y, core).
Axes of the slice: x: 2, y: 2, z: 4, core: 2. Of those that a mesh axis runs over, the one named last changes fastest.
Arguments:
- queries: bfloat16 [512, 5120], P(None, 'head'), may hold values from -18 to 18
- keys: bfloat16 [4096, 1024], P('ctx', 'head'), may hold values from -20 to 20
- values: bfloat16 [4096, 1024], P('ctx', 'head'), may hold values from -6 to 6
- stretch_lengths: int32 [32], replicated, may hold values from 1 to 512, 4096 in all
- query_pos: int32 [512], replicated, may hold values from 0 to 511, each once
Outputs:
- attended: bfloat16 [512, 5120], P('ctx', 'head')
- stretch_mass: float32 [32, 512], replicated
The draws below stay inside these ranges and needn't reach their ends.
Inputs may be any that keep to these rules, and one draw needn't show every extreme that they name: `stretch_lengths`: stretch lengths sum to 4096; the longest is exactly 512. `query_pos`: each of 0 to 511 appears once.
All inputs are finite; a program needn't handle non-finite values.
Results may differ from the reference program's by a relative error of at most 0.0076.
Values sent between devices are 32-bit elements; how exact they have to be, the bound alone decides.
No kernel may reach another device: no remote copies, remote signals or barrier semaphores. Data moves between devices by JAX's collectives and lax.ppermute only.
A program may use at most 64 MiB of HBM per device.

```python
import math
import jax
import jax.numpy as jnp
import numpy as np
from jax import lax

HQ = 40
KVH = 8
HD = 128
NQ = 512
TOK_DEV = 512
CTX_TOK = 4096
NCH = 32


def draw_queries(key, part):
    width = HQ * HD
    base = jnp.clip(3.0 * jax.random.normal(key, (NQ, width), jnp.float32), -18.0, 18.0)
    return base.astype(jnp.bfloat16)


def draw_keys(key, part):
    width = KVH * HD
    key_base = jax.random.fold_in(key, 0)
    base = jnp.clip(jax.random.normal(key_base, (CTX_TOK, width), jnp.float32), -6.0, 6.0)
    return base.astype(jnp.bfloat16)


def shard_levels(rng, dims, cuts, low, high):
    level, own = 1.0, jax.random.fold_in(rng, 6)
    for dim, parts in cuts:
        draws = jnp.exp(jax.random.uniform(jax.random.fold_in(own, dim), (parts,), jnp.float32, low / len(cuts), high / len(cuts)))
        level = level * jnp.repeat(draws, dims[dim] // parts).reshape([-1 if axis == dim else 1 for axis in range(len(dims))])
    return level


def split_up(amount, total, reach, skew):
    weights = [(1 << 20) // math.isqrt(rank ** skew) + 1 for rank in range(2, amount + 1)]
    rest, given = total - reach - (amount - 1), [1] * (amount - 1)
    while rest > 0:
        movable = [i for i in range(amount - 1) if given[i] < reach]
        mass, remaining = sum([weights[i] for i in movable]), rest
        for i in movable:
            extra = min(reach - given[i], max(1, remaining * weights[i] // mass), rest)
            given[i] = given[i] + extra
            rest = rest - extra
    return np.array([reach] + given)


def ragged(own_key, amount, total, bound, lean):
    if amount == 2:
        one = jax.random.randint(own_key, (), max(1, total - bound), min(bound, total - 1) + 1)
        return jnp.stack([one, total - one])
    sizes = jnp.asarray(split_up(amount, total, bound, lean), jnp.int32)
    twos = (amount - 1) // 2
    source_of, receiver = sizes[1:1 + 2 * twos:2], sizes[2:2 + 2 * twos:2]
    margin = jnp.minimum(source_of - 1, bound - receiver)
    passed = jax.random.randint(jax.random.fold_in(own_key, 1), (twos,), 0, 1 << 20) % (margin + 1)
    sizes = sizes.at[1:1 + 2 * twos:2].set(source_of - passed).at[2:2 + 2 * twos:2].set(receiver + passed)
    return sizes[jax.random.permutation(jax.random.fold_in(own_key, 2), amount)]


def bell_draw(stream_key, shape, spread, bound, cuts=(), kind=jnp.bfloat16):
    array = jax.random.normal(stream_key, shape, jnp.float32) * spread
    if len(cuts) > 0:
        array = shard_levels(stream_key, shape, cuts, -0.22, 0.18) * array
    return jnp.clip(array, min=-bound, max=bound).astype(kind)


def setup_inputs(seed: int = 0) -> dict:
    arg_keys = jax.random.split(jax.random.key(seed), 6)
    queries = draw_queries(jax.random.fold_in(arg_keys[5], 71), 0)
    keys = draw_keys(jax.random.fold_in(arg_keys[5], 71), 0)
    values = bell_draw(arg_keys[2], (CTX_TOK, KVH * HD), 1.0, 6.0, ((0, 8), (1, 4)))
    stretch_lengths = ragged(arg_keys[3], NCH, CTX_TOK, TOK_DEV, 1).astype(jnp.int32)
    query_pos = jax.random.permutation(arg_keys[4], NQ).astype(jnp.int32)
    return {"queries": queries, "keys": keys, "values": values, "stretch_lengths": stretch_lengths, "query_pos": query_pos}


ROPE_BASE = 1000000.0
floor_value = -1e30


def rope_queries(queries, query_pos):
    query_count = queries.shape[0]
    head_count = queries.shape[1] // HD
    half_dim = HD // 2
    frequency = ROPE_BASE ** (-(jnp.arange(half_dim, dtype=jnp.float32) * 2.0 / HD))
    angles = query_pos.astype(jnp.float32)[:, None] * frequency[None, :]
    cosine = jnp.cos(angles)[:, None, :]
    sin_part = jnp.sin(angles)[:, None, :]
    as_float = queries.astype(jnp.float32).reshape(query_count, head_count, HD)
    front_half = as_float[..., :half_dim]
    back_half = as_float[..., half_dim:]
    rotated = jnp.concatenate([front_half * cosine - back_half * sin_part, back_half * cosine + front_half * sin_part], axis=-1)
    return rotated.astype(jnp.bfloat16)


def reference(queries, keys, values, stretch_lengths, query_pos):
    roped = rope_queries(queries, query_pos)
    group_size = HQ // KVH
    query_heads = roped.reshape(NQ, KVH, group_size, HD).transpose(1, 2, 0, 3)
    key_heads = keys.reshape(CTX_TOK, KVH, HD).transpose(1, 0, 2)
    value_heads = values.reshape(CTX_TOK, KVH, HD).transpose(1, 0, 2)
    starts = jnp.cumsum(stretch_lengths) - stretch_lengths
    stretch_ends = starts + stretch_lengths
    key_block_len = math.gcd(CTX_TOK, 8192)
    block_count = CTX_TOK // key_block_len
    score_scale = HD ** -0.5

    def one_head(pieces):
        q_group, k_group, v_group = pieces
        q_float = q_group.astype(jnp.float32)
        key_blocks = k_group.reshape(block_count, key_block_len, HD)
        value_blocks = v_group.reshape(block_count, key_block_len, HD)

        def score_block(k_block):
            return jnp.einsum('jqd,kd->jqk', q_float, k_block.astype(jnp.float32)) * score_scale

        def first_pass(state_pair, k_block):
            row_top, row_sum = state_pair
            logits = score_block(k_block)
            new_top = jnp.maximum(row_top, logits.max(-1))
            row_sum = row_sum * jnp.exp(row_top - new_top) + jnp.sum(jnp.exp(logits - new_top[..., None]), axis=-1)
            return (new_top, row_sum), None

        start_top = jnp.full((group_size, NQ), floor_value, jnp.float32)
        start_sum = jnp.zeros((group_size, NQ), jnp.float32)
        (row_top, row_sum), _ = lax.scan(first_pass, (start_top, start_sum), key_blocks)

        def second_pass(state_pair, pieces_two):
            weighted, mass_sum = state_pair
            k_block, v_block, block_index = pieces_two
            logits = score_block(k_block)
            rounded = jnp.exp(logits - row_top[..., None]).astype(jnp.bfloat16).astype(jnp.float32)
            weighted = weighted + jnp.einsum('jqk,kd->jqd', rounded, v_block.astype(jnp.float32))
            share = jnp.sum(rounded / row_sum[..., None], axis=0)
            key_position = block_index * key_block_len + jnp.arange(key_block_len, dtype=jnp.int32)
            onehot = ((key_position[:, None] >= starts[None, :]) & (key_position[:, None] < stretch_ends[None, :])).astype(jnp.float32)
            mass_sum = mass_sum + jnp.dot(share, onehot, precision=lax.Precision.HIGHEST)
            return (weighted, mass_sum), None

        start_weighted = jnp.zeros((group_size, NQ, HD), jnp.float32)
        start_mass = jnp.zeros((NQ, NCH), jnp.float32)
        block_ids = jnp.arange(block_count, dtype=jnp.int32)
        (weighted, mass_sum), _ = lax.scan(second_pass, (start_weighted, start_mass), (key_blocks, value_blocks, block_ids))
        return weighted / row_sum[..., None], mass_sum

    head_outputs, head_masses = lax.map(one_head, (query_heads, key_heads, value_heads))
    attended = head_outputs.transpose(2, 0, 1, 3).reshape(NQ, HQ * HD).astype(jnp.bfloat16)
    stretch_mass = (jnp.sum(head_masses, axis=0) * (NCH / HQ)).T
    return attended, stretch_mass
```

```python
import functools
import math

import jax
import jax.numpy as jnp
from jax import lax
from jax.experimental import pallas as pl
from jax.experimental.pallas import tpu as pltpu
from jax.sharding import PartitionSpec as P

HD = 128
ROPE_BASE = 1000000.0
LOG2_SCALE = HD ** (-0.5) * math.log2(math.e)
VMEM_LIMIT = 40 * 1024 * 1024
STAT_ROWS = 16

CHUNKS = ((3, 0), (2, 1), (3, 0), (2, 0))
TIES = {}


def position(rel, order):
    place = 0
    for bit in order:
        place = place * 2 + ((rel // bit) & 1)
    return place


def blocks_in_order(order):
    return sorted(range(2 ** len(order)), key=lambda rel: position(rel, order))


def flash_kernel(
    order, first_head, group_size,
    where_ref, q_ref, k_ref, v_ref, cos_ref, sin_ref, lens_ref,
    keep_ref, send_ref, stats_ref, mass_ref, values_t, whole,
):
    step = pl.program_id(0)
    head = first_head + step
    tok_here = k_ref.shape[0]
    stretch_count = lens_ref.shape[1]
    me = where_ref[0]

    @pl.when(step == 0)
    def _():
        stats_ref[...] = jnp.zeros_like(stats_ref)
        lens = lens_ref[...].astype(jnp.float32)
        row = lax.broadcasted_iota(jnp.int32, (stretch_count, stretch_count), 0)
        column = lax.broadcasted_iota(jnp.int32, (stretch_count, stretch_count), 1)
        ends = jnp.sum(jnp.where(column <= row, lens, 0.0), axis=1, keepdims=True)
        starts = jnp.sum(jnp.where(column < row, lens, 0.0), axis=1, keepdims=True)
        at = lax.broadcasted_iota(jnp.int32, (stretch_count, tok_here), 1) + me * tok_here
        at = at.astype(jnp.float32)
        inside = (at >= starts) & (at < ends)
        values_t[HD:, :] = jnp.where(inside, 1.0, 0.0).astype(jnp.bfloat16)

    @pl.when((step == 0) | (lax.rem(head, group_size) == 0))
    def _():
        values_t[:HD, :] = v_ref[...].T

    q = q_ref[...].astype(jnp.float32)
    turned = pltpu.roll(q, HD // 2, axis=1)
    roped = (q * cos_ref[...] + turned * sin_ref[...]).astype(jnp.bfloat16)
    raw = lax.dot_general(
        k_ref[...], roped, (((1,), (1,)), ((), ())), preferred_element_type=jnp.float32
    )
    top = jnp.max(raw, axis=0, keepdims=True)
    weights = jnp.exp2((raw - top) * LOG2_SCALE)
    row_sum = jnp.sum(weights, axis=0, keepdims=True)
    stats_ref[pl.ds(step, 1), :] = top * LOG2_SCALE
    stats_ref[pl.ds(STAT_ROWS + step, 1), :] = row_sum
    out_t = jnp.dot(values_t[...], weights.astype(jnp.bfloat16), preferred_element_type=jnp.float32)
    mass_ref[...] = out_t[HD:]
    whole[...] = out_t[:HD].T
    blocks = blocks_in_order(order)
    rows = whole.shape[0] // len(blocks)
    half = len(blocks) // 2
    for place, rel in enumerate(blocks):
        source = pl.multiple_of((me ^ rel) * rows, rows)
        target = keep_ref if place < half else send_ref
        target[(place % half) * rows : (place % half + 1) * rows, :] = whole[pl.ds(source, rows), :]


def flash(order, first_head, head_count, group_size, where, queries, keys, values, cosine, sine, lens):
    query_count = queries.shape[0]
    tok_here = keys.shape[0]
    stretch_count = lens.shape[1]
    half = query_count // 2
    work = head_count * query_count * tok_here
    vmem = pl.BlockSpec(memory_space=pltpu.VMEM)
    kv_spec = pl.BlockSpec((tok_here, HD), lambda j: (0, (first_head + j) // group_size))
    return pl.pallas_call(
        functools.partial(flash_kernel, order, first_head, group_size),
        grid=(head_count,),
        in_specs=[
            pl.BlockSpec(memory_space=pltpu.SMEM),
            pl.BlockSpec((query_count, HD), lambda j: (0, first_head + j)),
            kv_spec,
            kv_spec,
            vmem,
            vmem,
            vmem,
        ],
        out_specs=[
            pl.BlockSpec((half, HD), lambda j: (0, j)),
            pl.BlockSpec((half, HD), lambda j: (0, j)),
            pl.BlockSpec((2 * STAT_ROWS, query_count), lambda j: (0, 0)),
            pl.BlockSpec((stretch_count, query_count), lambda j: (j, 0)),
        ],
        out_shape=[
            jax.ShapeDtypeStruct((half, head_count * HD), jnp.float32),
            jax.ShapeDtypeStruct((half, head_count * HD), jnp.float32),
            jax.ShapeDtypeStruct((2 * STAT_ROWS, query_count), jnp.float32),
            jax.ShapeDtypeStruct((head_count * stretch_count, query_count), jnp.float32),
        ],
        scratch_shapes=[
            pltpu.VMEM((HD + stretch_count, tok_here), jnp.bfloat16),
            pltpu.VMEM((query_count, HD), jnp.float32),
        ],
        compiler_params=pltpu.CompilerParams(vmem_limit_bytes=VMEM_LIMIT),
        cost_estimate=pl.CostEstimate(
            flops=work * 4 * HD, bytes_accessed=work, transcendentals=work
        ),
    )(where, queries, keys, values, cosine, sine, lens)


def weigh_kernel(orders, head_counts, factor, where_ref, own_ref, whole_ref, *refs):
    order_count = len(orders)
    tops_refs = refs[:order_count]
    mass_refs = refs[order_count : order_count + len(head_counts)]
    out_ref = refs[order_count + len(head_counts)]
    weight_refs = refs[order_count + len(head_counts) + 1 : -1]
    columns = refs[-1]
    me = where_ref[0]
    top, inverse = whole_ref[:STAT_ROWS], 1.0 / whole_ref[STAT_ROWS:]
    mine = jnp.exp2(own_ref[:STAT_ROWS] - top) * inverse
    stretch_count = out_ref.shape[0]
    total, head = None, 0
    for count, mass_ref in zip(head_counts, mass_refs):
        for j in range(count):
            term = mass_ref[j * stretch_count : (j + 1) * stretch_count] * mine[head : head + 1]
            total = term if total is None else total + term
            head += 1
    out_ref[...] = total * factor
    theirs = [jnp.exp2(tops_ref[...] - top) * inverse for tops_ref in tops_refs]
    filled = (1 + order_count) * STAT_ROWS
    rest = jnp.zeros((HD - filled, top.shape[1]), jnp.float32)
    columns[...] = jnp.concatenate([mine] + theirs + [rest], axis=0).T
    for order, weight_ref in zip(orders, weight_refs):
        blocks = blocks_in_order(order)
        rows = columns.shape[0] // len(blocks)
        for place, rel in enumerate(blocks[: len(blocks) // 2]):
            source = pl.multiple_of((me ^ rel) * rows, rows)
            weight_ref[place * rows : (place + 1) * rows, :] = columns[pl.ds(source, rows), :]


def weigh(orders, head_counts, factor, where, own, whole, tops, masses):
    query_count = own.shape[1]
    stretch_count = masses[0].shape[0] // head_counts[0]
    vmem = pl.BlockSpec(memory_space=pltpu.VMEM)
    return pl.pallas_call(
        functools.partial(weigh_kernel, orders, head_counts, factor),
        in_specs=[pl.BlockSpec(memory_space=pltpu.SMEM)] + [vmem] * (2 + len(tops) + len(masses)),
        out_specs=[vmem] * (1 + len(orders)),
        out_shape=[jax.ShapeDtypeStruct((stretch_count, query_count), jnp.float32)]
        + [jax.ShapeDtypeStruct((query_count // 2, HD), jnp.float32)] * len(orders),
        scratch_shapes=[pltpu.VMEM((query_count, HD), jnp.float32)],
        compiler_params=pltpu.CompilerParams(vmem_limit_bytes=VMEM_LIMIT),
        cost_estimate=pl.CostEstimate(flops=1 << 20, bytes_accessed=1 << 20, transcendentals=1 << 14),
    )(where, own, whole, *tops, *masses)


def merge_kernel(first_head, other, keep_ref, got_ref, weight_ref, near_ref, far_ref):
    half = near_ref.shape[0]
    for j in range(keep_ref.shape[1] // HD):
        columns = slice(j * HD, (j + 1) * HD)
        head = first_head + j
        theirs = (1 + other) * STAT_ROWS + head
        for rows, target in ((slice(0, half), near_ref), (slice(half, 2 * half), far_ref)):
            target[:, columns] = (
                keep_ref[rows, columns] * weight_ref[rows, head : head + 1]
                + got_ref[rows, columns] * weight_ref[rows, theirs : theirs + 1]
            )


def merge(first_head, other, keep, got, weights):
    rows, columns = keep.shape
    vmem = pl.BlockSpec(memory_space=pltpu.VMEM)
    return pl.pallas_call(
        functools.partial(merge_kernel, first_head, other),
        in_specs=[vmem] * 3,
        out_specs=[vmem] * 2,
        out_shape=[jax.ShapeDtypeStruct((rows // 2, columns), jnp.float32)] * 2,
        compiler_params=pltpu.CompilerParams(vmem_limit_bytes=VMEM_LIMIT),
        cost_estimate=pl.CostEstimate(
            flops=3 * rows * columns, bytes_accessed=12 * rows * columns, transcendentals=0
        ),
    )(keep, got, weights)


def join_stats(one, two):
    top = jnp.maximum(one[:STAT_ROWS], two[:STAT_ROWS])
    total = one[STAT_ROWS:] * jnp.exp2(one[:STAT_ROWS] - top) + two[STAT_ROWS:] * jnp.exp2(
        two[:STAT_ROWS] - top
    )
    return jnp.concatenate([top, total], axis=0)


def local(queries, keys, values, stretch_lengths, query_pos):
    query_count = queries.shape[0]
    heads_here = queries.shape[1] // HD
    group_size = heads_here // (keys.shape[1] // HD)
    stretch_count = stretch_lengths.shape[0]
    ctx_size, head_size = lax.axis_size("ctx"), lax.axis_size("head")
    where = lax.axis_index("ctx").astype(jnp.int32).reshape(1)
    bits = tuple(2**i for i in range(ctx_size.bit_length() - 1))
    done = {}

    def swap(name, array, axis, bit):
        size = lax.axis_size(axis)
        waits = [done[other] for other in TIES.get(name, ()) if other in done]
        if waits:
            array = lax.optimization_barrier((array, *waits))[0]
        done[name] = lax.ppermute(array, axis, [(i, i ^ bit) for i in range(size)])
        return done[name]

    half_dim = HD // 2
    frequency = ROPE_BASE ** (-(jnp.arange(half_dim, dtype=jnp.float32) * 2.0 / HD))
    angles = query_pos.astype(jnp.float32)[:, None] * frequency[None, :]
    cosine, sine = jnp.cos(angles), jnp.sin(angles)
    cosine = jnp.concatenate([cosine, cosine], axis=1)
    sine = jnp.concatenate([-sine, sine], axis=1)
    lens = stretch_lengths.reshape(1, stretch_count)

    orders = {}
    chunks = []
    first_head = 0
    for head_count, turn in CHUNKS:
        order = bits[turn:] + bits[:turn]
        keep, send, stats, masses = flash(
            order, first_head, head_count, group_size, where, queries, keys, values, cosine, sine, lens
        )
        orders.setdefault(order, len(orders))
        name = "c%d" % len(chunks)
        got = swap("%s.%d" % (name, order[0]), send, "ctx", order[0])
        chunks.append((name, order, first_head, head_count, keep, got, stats, masses))
        first_head += head_count

    pad = jnp.zeros((STAT_ROWS - heads_here, query_count), jnp.float32)
    tops = [c[6][: c[3]] for c in chunks] + [pad]
    sums = [c[6][STAT_ROWS : STAT_ROWS + c[3]] for c in chunks] + [pad + 1.0]
    own = jnp.concatenate(tops + sums, axis=0)
    joined, partner_tops = own, {}
    firsts = [order[0] for order in orders]
    for bit in bits:
        message = joined
        if bit in firsts and bit != bits[0]:
            message = jnp.concatenate([joined, own[:STAT_ROWS]], axis=0)
        got = swap("a.%d" % bit, message, "ctx", bit)
        if bit in firsts:
            partner_tops[bit] = got[:STAT_ROWS] if bit == bits[0] else got[2 * STAT_ROWS :]
        joined = join_stats(joined, got[: 2 * STAT_ROWS])

    factor = stretch_count / (heads_here * head_size)
    mass, *weights = weigh(
        tuple(orders), tuple(c[3] for c in chunks), factor, where, own, joined,
        [partner_tops[bit] for bit in firsts], [c[7] for c in chunks],
    )

    for bit in (2**i for i in range(head_size.bit_length() - 1)):
        mass = mass + swap("mh.%d" % bit, mass, "head", bit)
    for bit in bits:
        mass = mass + swap("m.%d" % bit, mass, "ctx", bit)

    state = []
    for name, order, first_head, head_count, keep, got, _, _ in chunks:
        kind = orders[order]
        state.append(merge(first_head, kind, keep, got, weights[kind]))
    for i in range(1, len(bits)):
        for n, (name, order, *_) in enumerate(chunks):
            keep, send = state[n]
            keep = keep + swap("%s.%d" % (name, order[i]), send, "ctx", order[i])
            if i < len(bits) - 1:
                rows = keep.shape[0] // 2
                state[n] = (keep[:rows], keep[rows:])
            else:
                state[n] = keep
    attended = jnp.concatenate([part.astype(jnp.bfloat16) for part in state], axis=1)
    return attended, mass


def solution(mesh):
    placed = (P(None, "head"), P("ctx", "head"), P("ctx", "head"), P(), P())
    return jax.shard_map(
        local, mesh=mesh, in_specs=placed, out_specs=(P("ctx", "head"), P()), check_vma=False
    )
```

```python
import functools
import math

import jax
import jax.numpy as jnp
import numpy as np
from jax import lax
from jax.experimental import pallas as pl
from jax.experimental.pallas import tpu as pltpu
from jax.sharding import PartitionSpec as P

HD = 128
ROPE_BASE = 1000000.0
LOG2_SCALE = HD ** (-0.5) * math.log2(math.e)
VMEM_LIMIT = 16 * 1024 * 1024
FLASH_VMEM = 60 * 1024 * 1024
STAT_ROWS = 16
TILE = 128
HALF_PI = (1.5706787109375, 1.1761486530303955e-4, 9.920935796805404e-10)

CHUNKS = ((4, 0), (1, 1), (4, 0), (1, 1))
TIES = {
    "c0.2": ("c1.2",),
    "m.2": ("c0.2",),
    "c1.1": ("a.4",),
    "m.1": ("h.2",),
    "c3.4": ("c0.1",),
}
FENCES = ()
MASS_ORDER = ("h.1", "h.2", "m.1", "m.2", "m.4")


def position(rel, order):
    place = 0
    for bit in order:
        place = place * 2 + ((rel // bit) & 1)
    return place


def blocks_in_order(order):
    return sorted(range(2 ** len(order)), key=lambda rel: position(rel, order))


def rope_tables(pos_ref, frequency_ref, cos_ref, sin_ref):
    query_count = cos_ref.shape[0]
    half = query_count // 2
    rows = []
    for group in range(query_count // HD):
        row = pos_ref[group : group + 1, :].astype(jnp.float32)
        rows.append(jnp.broadcast_to(row, (HD, HD)).T)
    places = jnp.concatenate(rows, axis=0)
    left = lax.broadcasted_iota(jnp.int32, (1, HD), 1) < HD // 2
    angle = jnp.where(left, places[:half], places[half:]) * frequency_ref[...]
    turns = jnp.floor(angle * (2.0 / math.pi) + 0.5)
    rest = ((angle - turns * HALF_PI[0]) - turns * HALF_PI[1]) - turns * HALF_PI[2]
    square = rest * rest
    sine = rest + rest * square * (
        -1.6666654611e-1 + square * (8.3321608736e-3 + square * -1.9515295891e-4)
    )
    cosine = (1.0 - 0.5 * square) + square * square * (
        4.166664568298827e-2 + square * (-1.388731625493765e-3 + square * 2.443315711809948e-5)
    )
    quarter = turns.astype(jnp.int32) & 3
    odd = (quarter & 1) == 1
    cos_value = jnp.where(odd, sine, cosine) * jnp.where((quarter == 1) | (quarter == 2), -1.0, 1.0)
    sin_value = jnp.where(odd, cosine, sine) * jnp.where(quarter >= 2, -1.0, 1.0)
    cos_other = pltpu.roll(cos_value, HD // 2, axis=1)
    sin_other = pltpu.roll(sin_value, HD // 2, axis=1)
    cos_ref[:half, :] = jnp.where(left, cos_value, cos_other)
    cos_ref[half:, :] = jnp.where(left, cos_other, cos_value)
    sin_ref[:half, :] = jnp.where(left, -sin_value, sin_other)
    sin_ref[half:, :] = jnp.where(left, -sin_other, sin_value)


def flash_kernel(parts, group_size, slots, lens_ref, pos_ref, frequency_ref, q_hbm, k_hbm, v_hbm, *refs):
    refs = list(refs)
    keeps = [refs.pop(0) for _ in parts]
    sends = [refs.pop(0) for _ in parts]
    mass_hbm, stats_ref = refs.pop(0), refs.pop(0)
    q_ref, k_ref, v_ref, cos_ref, sin_ref, values, whole, halves, mass_ref, columns = refs[:10]
    kv_sems, half_sems, mass_sems = refs[10:]
    query_count, tok_here = q_ref.shape[0], k_ref.shape[0]
    stretch_count = lens_ref.shape[0]
    me = lax.axis_index("ctx")
    head_count = sum(count for _, count in parts)
    kv_count = head_count // group_size
    width = slots * stretch_count

    k_copy = pltpu.make_async_copy(k_hbm, k_ref, kv_sems.at[0])
    v_copy = pltpu.make_async_copy(v_hbm, v_ref, kv_sems.at[1])
    k_copy.start()
    q_copy = pltpu.make_async_copy(q_hbm, q_ref, kv_sems.at[2])
    q_copy.start()
    v_copy.start()

    rope_tables(pos_ref, frequency_ref, cos_ref, sin_ref)
    lane = lax.broadcasted_iota(jnp.int32, columns.shape, 1)
    columns[...] = jnp.where(lane < STAT_ROWS, 0.0, 1.0)
    lane = lax.broadcasted_iota(jnp.int32, (1, width), 1)
    starts, ends = jnp.zeros((1, width), jnp.int32), jnp.zeros((1, width), jnp.int32)
    edge = -me * tok_here
    for c in range(stretch_count):
        here = (lane & (stretch_count - 1)) == c
        starts = jnp.where(here, edge, starts)
        edge = edge + lens_ref[c]
        ends = jnp.where(here, edge, ends)
    at = lax.broadcasted_iota(jnp.int32, (tok_here, width), 0)
    inside = jnp.where((at >= starts) & (at < ends), 1.0, 0.0)
    slot_of_lane = lane // stretch_count
    for slot in range(slots):
        marks = jnp.where(slot_of_lane == slot, inside, 0.0).astype(jnp.bfloat16)
        for g in range(kv_count):
            values[g, slot, :, HD:] = marks
    v_copy.wait()
    for g in range(kv_count):
        for slot in range(slots):
            values[g, slot, :, :HD] = v_ref[:, g * HD : (g + 1) * HD]
    k_copy.wait()
    q_copy.wait()

    tile = min(TILE, query_count)
    half_copies, mass_copies = [], []
    for j in range(head_count):
        g = j // group_size
        lanes = slice(j // slots * width, (j // slots + 1) * width)
        for t in range(query_count // tile):
            rows = slice(t * tile, (t + 1) * tile)
            q = q_ref[rows, j * HD : (j + 1) * HD].astype(jnp.float32)
            turned = pltpu.roll(q, HD // 2, axis=1)
            roped = (q * cos_ref[rows, :] + turned * sin_ref[rows, :]).astype(jnp.bfloat16)
            raw = lax.dot_general(
                roped, k_ref[:, g * HD : (g + 1) * HD], (((1,), (1,)), ((), ())),
                preferred_element_type=jnp.float32,
            )
            top = jnp.max(raw, axis=1, keepdims=True)
            weights = jnp.exp2((raw - top) * LOG2_SCALE)
            columns[rows, j : j + 1] = top
            columns[rows, STAT_ROWS + j : STAT_ROWS + j + 1] = jnp.sum(weights, axis=1, keepdims=True)
            out = jnp.dot(
                weights.astype(jnp.bfloat16), values[g, j % slots], preferred_element_type=jnp.float32
            )
            whole[j % 2, rows, :] = out[:, :HD]
            if j % slots == 0:
                mass_ref[rows, lanes] = out[:, HD:]
            else:
                mass_ref[rows, lanes] += out[:, HD:]
        part, local_head = 0, j
        while local_head >= parts[part][1]:
            local_head -= parts[part][1]
            part += 1
        blocks = blocks_in_order(parts[part][0])
        size = query_count // len(blocks)
        half = len(blocks) // 2
        for place, rel in enumerate(blocks):
            source = pl.multiple_of((me ^ rel) * size, size)
            side, place = place // half, place % half
            halves[j, side, place * size : (place + 1) * size, :] = whole[j % 2, pl.ds(source, size), :]
        if local_head == parts[part][1] - 1:
            first_head = j - local_head
            for i in range(first_head, j + 1):
                lanes = pl.ds((i - first_head) * HD, HD)
                for side, target in ((0, keeps[part]), (1, sends[part])):
                    half_copies.append(
                        pltpu.make_async_copy(
                            halves.at[i, side], target.at[:, lanes], half_sems.at[i, side]
                        )
                    )
                    half_copies[-1].start()
    for group in range(-(-head_count // slots)):
        lanes = pl.ds(group * width, width)
        mass_copies.append(
            pltpu.make_async_copy(mass_ref.at[:, lanes], mass_hbm.at[:, lanes], mass_sems.at[group])
        )
        mass_copies[-1].start()
    stats_ref[...] = columns[...].T[: 2 * STAT_ROWS]
    for copy in half_copies + mass_copies:
        copy.wait()


def flash(parts, group_size, queries, keys, values, lens, places, frequency):
    query_count = queries.shape[0]
    tok_here = keys.shape[0]
    stretch_count = lens.shape[0]
    head_count = sum(count for _, count in parts)
    half = query_count // 2
    slots = max(1, HD // stretch_count)
    width = slots * stretch_count
    groups = -(-head_count // slots)
    work = head_count * query_count * tok_here
    vmem = pl.BlockSpec(memory_space=pltpu.VMEM)
    hbm = pl.BlockSpec(memory_space=pltpu.HBM)
    halves = [jax.ShapeDtypeStruct((half, count * HD), jnp.float32) for _, count in parts]
    mass = jax.ShapeDtypeStruct((query_count, groups * width), jnp.float32)
    stats = jax.ShapeDtypeStruct((2 * STAT_ROWS, query_count), jnp.float32)
    return pl.pallas_call(
        functools.partial(flash_kernel, parts, group_size, slots),
        in_specs=[pl.BlockSpec(memory_space=pltpu.SMEM), vmem, vmem, hbm, hbm, hbm],
        out_specs=[hbm] * (2 * len(parts) + 1) + [vmem],
        out_shape=halves + halves + [mass, stats],
        scratch_shapes=[
            pltpu.VMEM(queries.shape, jnp.bfloat16),
            pltpu.VMEM(keys.shape, jnp.bfloat16),
            pltpu.VMEM(values.shape, jnp.bfloat16),
            pltpu.VMEM((query_count, HD), jnp.float32),
            pltpu.VMEM((query_count, HD), jnp.float32),
            pltpu.VMEM((head_count // group_size, slots, tok_here, HD + width), jnp.bfloat16),
            pltpu.VMEM((2, query_count, HD), jnp.float32),
            pltpu.VMEM((head_count, 2, half, HD), jnp.float32),
            pltpu.VMEM(mass.shape, jnp.float32),
            pltpu.VMEM((query_count, HD), jnp.float32),
            pltpu.SemaphoreType.DMA((3,)),
            pltpu.SemaphoreType.DMA((head_count, 2)),
            pltpu.SemaphoreType.DMA((groups,)),
        ],
        compiler_params=pltpu.CompilerParams(vmem_limit_bytes=FLASH_VMEM),
        cost_estimate=pl.CostEstimate(
            flops=work * 4 * HD, bytes_accessed=work, transcendentals=work
        ),
    )(lens, places, frequency, queries, keys, values)


def weigh_kernel(orders, head_counts, factor, own_ref, whole_ref, *refs):
    order_count = len(orders)
    tops_refs = refs[:order_count]
    mass_refs = refs[order_count : order_count + len(head_counts)]
    out_ref = refs[order_count + len(head_counts)]
    weight_refs = refs[order_count + len(head_counts) + 1 : -1]
    columns = refs[-1]
    me = lax.axis_index("ctx")
    top, inverse = whole_ref[:STAT_ROWS], 1.0 / whole_ref[STAT_ROWS:]
    mine = jnp.exp2(own_ref[:STAT_ROWS] - top) * inverse
    stretch_count = out_ref.shape[0]
    slots = max(1, HD // stretch_count)
    width = slots * stretch_count
    total, head = None, 0
    for count, mass_ref in zip(head_counts, mass_refs):
        for j in range(count):
            if j % slots == 0:
                turned = mass_ref[:, j // slots * width : (j // slots + 1) * width].T
            at = j % slots * stretch_count
            term = turned[at : at + stretch_count] * mine[head : head + 1]
            total = term if total is None else total + term
            head += 1
    out_ref[...] = total * factor
    theirs = [jnp.exp2(tops_ref[...] - top) * inverse for tops_ref in tops_refs]
    filled = (1 + order_count) * STAT_ROWS
    rest = jnp.zeros((HD - filled, top.shape[1]), jnp.float32)
    columns[...] = jnp.concatenate([mine] + theirs + [rest], axis=0).T
    for order, weight_ref in zip(orders, weight_refs):
        blocks = blocks_in_order(order)
        rows = columns.shape[0] // len(blocks)
        for place, rel in enumerate(blocks[: len(blocks) // 2]):
            source = pl.multiple_of((me ^ rel) * rows, rows)
            weight_ref[place * rows : (place + 1) * rows, :] = columns[pl.ds(source, rows), :]


def weigh(orders, head_counts, stretch_count, factor, own, whole, tops, masses):
    query_count = own.shape[1]
    vmem = pl.BlockSpec(memory_space=pltpu.VMEM)
    return pl.pallas_call(
        functools.partial(weigh_kernel, orders, head_counts, factor),
        in_specs=[vmem] * (2 + len(tops) + len(masses)),
        out_specs=[vmem] * (1 + len(orders)),
        out_shape=[jax.ShapeDtypeStruct((stretch_count, query_count), jnp.float32)]
        + [jax.ShapeDtypeStruct((query_count // 2, HD), jnp.float32)] * len(orders),
        scratch_shapes=[pltpu.VMEM((query_count, HD), jnp.float32)],
        compiler_params=pltpu.CompilerParams(vmem_limit_bytes=VMEM_LIMIT),
        cost_estimate=pl.CostEstimate(flops=1 << 20, bytes_accessed=1 << 20, transcendentals=1 << 14),
    )(own, whole, *tops, *masses)


def merge_kernel(first_head, other, keep_ref, got_ref, weight_ref, near_ref, far_ref):
    half = near_ref.shape[0]
    for j in range(keep_ref.shape[1] // HD):
        columns = slice(j * HD, (j + 1) * HD)
        head = first_head + j
        theirs = (1 + other) * STAT_ROWS + head
        for rows, target in ((slice(0, half), near_ref), (slice(half, 2 * half), far_ref)):
            target[:, columns] = (
                keep_ref[rows, columns] * weight_ref[rows, head : head + 1]
                + got_ref[rows, columns] * weight_ref[rows, theirs : theirs + 1]
            )


def merge(first_head, other, keep, got, weights):
    rows, columns = keep.shape
    vmem = pl.BlockSpec(memory_space=pltpu.VMEM)
    return pl.pallas_call(
        functools.partial(merge_kernel, first_head, other),
        in_specs=[vmem] * 3,
        out_specs=[vmem] * 2,
        out_shape=[jax.ShapeDtypeStruct((rows // 2, columns), jnp.float32)] * 2,
        compiler_params=pltpu.CompilerParams(vmem_limit_bytes=VMEM_LIMIT),
        cost_estimate=pl.CostEstimate(
            flops=3 * rows * columns, bytes_accessed=12 * rows * columns, transcendentals=0
        ),
    )(keep, got, weights)


def in_log2(stats):
    return jnp.concatenate([stats[:STAT_ROWS] * LOG2_SCALE, stats[STAT_ROWS:]], axis=0)


def join_stats(one, two):
    top = jnp.maximum(one[:STAT_ROWS], two[:STAT_ROWS])
    total = one[STAT_ROWS:] * jnp.exp2(one[:STAT_ROWS] - top) + two[STAT_ROWS:] * jnp.exp2(
        two[:STAT_ROWS] - top
    )
    return jnp.concatenate([top, total], axis=0)


def local(queries, keys, values, stretch_lengths, query_pos):
    query_count = queries.shape[0]
    heads_here = queries.shape[1] // HD
    group_size = heads_here // (keys.shape[1] // HD)
    stretch_count = stretch_lengths.shape[0]
    ctx_size, head_size = lax.axis_size("ctx"), lax.axis_size("head")
    bits = tuple(2**i for i in range(ctx_size.bit_length() - 1))
    head_bits = tuple(2**i for i in range(head_size.bit_length() - 1))
    results = {}

    def once(make):
        @functools.wraps(make)
        def cached(*key):
            if (make.__name__, *key) not in results:
                results[(make.__name__, *key)] = make(*key)
            return results[(make.__name__, *key)]

        return cached

    def exchange(array, axis, bit):
        return lax.ppermute(array, axis, [(i, i ^ bit) for i in range(lax.axis_size(axis))])

    def after(names, arrays):
        waits = [arrived(other) for name in names for other in TIES.get(name, ()) if known(other)]
        return lax.optimization_barrier((*arrays, *waits))[: len(arrays)] if waits else arrays

    def run(names, step, state):
        state = tuple(after(names, state))
        if names not in FENCES:
            return step(names[0], *state)

        def steps(*state):
            for name in names:
                state = step(name, *state)
            return state

        return lax.cond(stretch_lengths[0] > 0, steps, lambda *state: state, *state)

    def runs(names):
        fences = [tuple(name for name in fence if name in names) for fence in FENCES]
        fences = [fence for fence in fences if fence]
        fenced = {name for fence in fences for name in fence}
        starts = {fence[0]: fence for fence in fences}
        return [starts.get(name, (name,)) for name in names if name in starts or name not in fenced]

    lane = np.arange(HD) % (HD // 2)
    frequency = jnp.asarray((ROPE_BASE ** (-2.0 * lane / HD)).astype(np.float32).reshape(1, HD))
    places = query_pos.reshape(query_count // HD, HD)
    parts = []
    for count, turn in CHUNKS:
        rotated = bits[turn:] + bits[:turn]
        first = bits[-turn]
        moved = (first,) + tuple(bit for bit in bits if bit != first)
        parts.append((rotated if turn >= 0 else moved, count))
    parts = tuple(parts)
    mass_steps = ["h.%d" % bit for bit in head_bits] + ["m.%d" % bit for bit in bits]
    mass_steps.sort(key=lambda name: MASS_ORDER.index(name) if name in MASS_ORDER else len(MASS_ORDER))
    orders = {}
    for order, _ in parts:
        orders.setdefault(order, len(orders))
    *halves, masses, raw_stats = flash(
        parts, group_size, queries, keys, values, stretch_lengths, places, frequency
    )
    keeps, sends = halves[: len(parts)], halves[len(parts) :]
    own = lax.optimization_barrier(in_log2(raw_stats))
    firsts = [order[0] for order in orders]

    def known(name):
        kind, bit = name.split(".")
        if kind == "h":
            return int(bit) in head_bits
        return int(bit) in bits

    stat_steps = ["a.%d" % bit for bit in bits]
    stat_runs, mass_runs = runs(stat_steps), runs(mass_steps)
    run_of = {name: i for names in (stat_runs, mass_runs) for i, run_ in enumerate(names) for name in run_}

    @once
    def arrived(name):
        kind, bit = name.split(".")
        if kind == "a":
            return stats(run_of[name] + 1)[0]
        if kind in ("h", "m"):
            return mass(run_of[name] + 1)[0]
        n, bit = int(kind[1:]), int(bit)
        i = parts[n][0].index(bit)
        send = sends[n] if i == 0 else halved(n, i)[1]
        return exchange(after([name], (send,))[0], "ctx", bit)

    def stat_step(name, joined, *tops):
        bit = int(name.split(".")[1])
        opening = bit == bits[0]
        message = raw_stats if opening else joined
        if bit in firsts and not opening:
            message = jnp.concatenate([message, own[:STAT_ROWS]], axis=0)
        got = exchange(message, "ctx", bit)
        joined = join_stats(joined, in_log2(got) if opening else got[: 2 * STAT_ROWS])
        if bit in firsts:
            top = got[:STAT_ROWS] * LOG2_SCALE if opening else got[2 * STAT_ROWS :]
            tops = tuple(top if i == firsts.index(bit) else old for i, old in enumerate(tops))
        return (joined, *tops)

    def mass_step(name, total):
        kind, bit = name.split(".")
        return (total + exchange(total, "head" if kind == "h" else "ctx", int(bit)),)

    @once
    def stats(step):
        if step == 0:
            return (own,) + (own[:STAT_ROWS],) * len(firsts)
        return run(stat_runs[step - 1], stat_step, stats(step - 1))

    @once
    def weighed():
        joined, *tops = stats(len(stat_runs))
        factor = stretch_count / (heads_here * head_size)
        return weigh(tuple(orders), (heads_here,), stretch_count, factor, own, joined, tops, [masses])

    @once
    def mass(step):
        if step == 0:
            return (weighed()[0],)
        return run(mass_runs[step - 1], mass_step, mass(step - 1))

    @once
    def halved(n, i):
        order, count = parts[n]
        got = arrived("c%d.%d" % (n, order[i - 1]))
        if i == 1:
            first_head = sum(c for _, c in parts[:n])
            kind = orders[order]
            return merge(first_head, kind, keeps[n], got, weighed()[1 + kind])
        total = halved(n, i - 1)[0] + got
        if i == len(order):
            return total
        rows = total.shape[0] // 2
        return total[:rows], total[rows:]

    done = [halved(n, len(bits)).astype(jnp.bfloat16) for n in range(len(parts))]
    return jnp.concatenate(done, axis=1), mass(len(mass_runs))[0]


def solution(mesh):
    placed = (P(None, "head"), P("ctx", "head"), P("ctx", "head"), P(), P())
    return jax.shard_map(
        local, mesh=mesh, in_specs=placed, out_specs=(P("ctx", "head"), P()), check_vma=False
    )
```

```python
import functools
import math

import jax
import jax.numpy as jnp
import numpy as np
from jax import lax
from jax.experimental import pallas as pl
from jax.experimental.pallas import tpu as pltpu
from jax.sharding import PartitionSpec as P

HD = 128
ROPE_BASE = 1000000.0
LOG2_SCALE = HD ** (-0.5) * math.log2(math.e)
VMEM_LIMIT = 16 * 1024 * 1024
FLASH_VMEM = 60 * 1024 * 1024
STAT_ROWS = 16
TILE = 128
HALF_PI = (1.5706787109375, 1.1761486530303955e-4, 9.920935796805404e-10)

CHUNKS = ((4, 0), (4, 0), (2, 1))
TIES = {"c1.1": ("a.2",), "c2.2": ("a.2",), "h.1": ("c0.1",)}
FENCES = (("a.2",),)
MASS_ORDER = ("h.1", "h.2", "m.1", "m.4", "m.2")


def position(rel, order):
    place = 0
    for bit in order:
        place = place * 2 + ((rel // bit) & 1)
    return place


def blocks_in_order(order):
    return sorted(range(2 ** len(order)), key=lambda rel: position(rel, order))


def rope_tables(pos_ref, frequency_ref, cos_ref, sin_ref):
    query_count = cos_ref.shape[0]
    half = query_count // 2
    rows = []
    for group in range(query_count // HD):
        row = pos_ref[group : group + 1, :].astype(jnp.float32)
        rows.append(jnp.broadcast_to(row, (HD, HD)).T)
    places = jnp.concatenate(rows, axis=0)
    left = lax.broadcasted_iota(jnp.int32, (1, HD), 1) < HD // 2
    angle = jnp.where(left, places[:half], places[half:]) * frequency_ref[...]
    turns = jnp.floor(angle * (2.0 / math.pi) + 0.5)
    rest = ((angle - turns * HALF_PI[0]) - turns * HALF_PI[1]) - turns * HALF_PI[2]
    square = rest * rest
    sine = rest + rest * square * (
        -1.6666654611e-1 + square * (8.3321608736e-3 + square * -1.9515295891e-4)
    )
    cosine = (1.0 - 0.5 * square) + square * square * (
        4.166664568298827e-2 + square * (-1.388731625493765e-3 + square * 2.443315711809948e-5)
    )
    quarter = turns.astype(jnp.int32) & 3
    odd = (quarter & 1) == 1
    cos_value = jnp.where(odd, sine, cosine) * jnp.where((quarter == 1) | (quarter == 2), -1.0, 1.0)
    sin_value = jnp.where(odd, cosine, sine) * jnp.where(quarter >= 2, -1.0, 1.0)
    cos_other = pltpu.roll(cos_value, HD // 2, axis=1)
    sin_other = pltpu.roll(sin_value, HD // 2, axis=1)
    cos_ref[:half, :] = jnp.where(left, cos_value, cos_other)
    cos_ref[half:, :] = jnp.where(left, cos_other, cos_value)
    sin_ref[:half, :] = jnp.where(left, -sin_value, sin_other)
    sin_ref[half:, :] = jnp.where(left, -sin_other, sin_value)


def flash_kernel(parts, group_size, slots, lens_ref, pos_ref, frequency_ref, q_hbm, k_hbm, v_hbm, *refs):
    refs = list(refs)
    keeps = [refs.pop(0) for _ in parts]
    sends = [refs.pop(0) for _ in parts]
    mass_hbm, stats_ref = refs.pop(0), refs.pop(0)
    q_ref, k_ref, v_ref, cos_ref, sin_ref, values, whole, halves, mass_ref, columns = refs[:10]
    kv_sems, half_sems, mass_sems = refs[10:]
    query_count, tok_here = q_ref.shape[0], k_ref.shape[0]
    stretch_count = lens_ref.shape[0]
    me = lax.axis_index("ctx")
    head_count = sum(count for _, count in parts)
    kv_count = head_count // group_size
    width = slots * stretch_count

    k_copy = pltpu.make_async_copy(k_hbm, k_ref, kv_sems.at[0])
    v_copy = pltpu.make_async_copy(v_hbm, v_ref, kv_sems.at[1])
    k_copy.start()
    q_copies = []
    for g in range(kv_count):
        lanes = pl.ds(g * group_size * HD, group_size * HD)
        q_copies.append(
            pltpu.make_async_copy(q_hbm.at[:, lanes], q_ref.at[:, lanes], kv_sems.at[2 + g])
        )
    q_copies[0].start()
    v_copy.start()
    for copy in q_copies[1:]:
        copy.start()

    rope_tables(pos_ref, frequency_ref, cos_ref, sin_ref)
    lane = lax.broadcasted_iota(jnp.int32, columns.shape, 1)
    columns[...] = jnp.where(lane < STAT_ROWS, 0.0, 1.0)
    lane = lax.broadcasted_iota(jnp.int32, (1, width), 1)
    starts, ends = jnp.zeros((1, width), jnp.int32), jnp.zeros((1, width), jnp.int32)
    edge = -me * tok_here
    for c in range(stretch_count):
        here = (lane & (stretch_count - 1)) == c
        starts = jnp.where(here, edge, starts)
        edge = edge + lens_ref[c]
        ends = jnp.where(here, edge, ends)
    at = lax.broadcasted_iota(jnp.int32, (tok_here, width), 0)
    inside = jnp.where((at >= starts) & (at < ends), 1.0, 0.0)
    slot_of_lane = lane // stretch_count
    for slot in range(slots):
        marks = jnp.where(slot_of_lane == slot, inside, 0.0).astype(jnp.bfloat16)
        for g in range(kv_count):
            values[g, slot, :, HD:] = marks
    v_copy.wait()
    for g in range(kv_count):
        for slot in range(slots):
            values[g, slot, :, :HD] = v_ref[:, g * HD : (g + 1) * HD]
    k_copy.wait()

    tile = min(TILE, query_count)
    half_copies, mass_copies = [], []
    for j in range(head_count):
        g = j // group_size
        if j % group_size == 0:
            q_copies[g].wait()
        lanes = slice(j // slots * width, (j // slots + 1) * width)
        for t in range(query_count // tile):
            rows = slice(t * tile, (t + 1) * tile)
            q = q_ref[rows, j * HD : (j + 1) * HD].astype(jnp.float32)
            turned = pltpu.roll(q, HD // 2, axis=1)
            roped = (q * cos_ref[rows, :] + turned * sin_ref[rows, :]).astype(jnp.bfloat16)
            raw = lax.dot_general(
                roped, k_ref[:, g * HD : (g + 1) * HD], (((1,), (1,)), ((), ())),
                preferred_element_type=jnp.float32,
            )
            top = jnp.max(raw, axis=1, keepdims=True)
            weights = jnp.exp2((raw - top) * LOG2_SCALE)
            columns[rows, j : j + 1] = top
            columns[rows, STAT_ROWS + j : STAT_ROWS + j + 1] = jnp.sum(weights, axis=1, keepdims=True)
            out = jnp.dot(
                weights.astype(jnp.bfloat16), values[g, j % slots], preferred_element_type=jnp.float32
            )
            whole[j % 2, rows, :] = out[:, :HD]
            if j % slots == 0:
                mass_ref[rows, lanes] = out[:, HD:]
            else:
                mass_ref[rows, lanes] += out[:, HD:]
        part, local_head = 0, j
        while local_head >= parts[part][1]:
            local_head -= parts[part][1]
            part += 1
        blocks = blocks_in_order(parts[part][0])
        size = query_count // len(blocks)
        half = len(blocks) // 2
        for place, rel in enumerate(blocks):
            source = pl.multiple_of((me ^ rel) * size, size)
            side, place = place // half, place % half
            halves[j, side, place * size : (place + 1) * size, :] = whole[j % 2, pl.ds(source, size), :]
        if local_head == parts[part][1] - 1:
            first_head = j - local_head
            for i in range(first_head, j + 1):
                lanes = pl.ds((i - first_head) * HD, HD)
                for side, target in ((0, keeps[part]), (1, sends[part])):
                    half_copies.append(
                        pltpu.make_async_copy(
                            halves.at[i, side], target.at[:, lanes], half_sems.at[i, side]
                        )
                    )
                    half_copies[-1].start()
    for group in range(-(-head_count // slots)):
        lanes = pl.ds(group * width, width)
        mass_copies.append(
            pltpu.make_async_copy(mass_ref.at[:, lanes], mass_hbm.at[:, lanes], mass_sems.at[group])
        )
        mass_copies[-1].start()
    stats_ref[...] = columns[...].T[: 2 * STAT_ROWS]
    for copy in half_copies + mass_copies:
        copy.wait()


def flash(parts, group_size, queries, keys, values, lens, places, frequency):
    query_count = queries.shape[0]
    tok_here = keys.shape[0]
    stretch_count = lens.shape[0]
    head_count = sum(count for _, count in parts)
    half = query_count // 2
    slots = max(1, HD // stretch_count)
    width = slots * stretch_count
    groups = -(-head_count // slots)
    work = head_count * query_count * tok_here
    vmem = pl.BlockSpec(memory_space=pltpu.VMEM)
    hbm = pl.BlockSpec(memory_space=pltpu.HBM)
    halves = [jax.ShapeDtypeStruct((half, count * HD), jnp.float32) for _, count in parts]
    mass = jax.ShapeDtypeStruct((query_count, groups * width), jnp.float32)
    stats = jax.ShapeDtypeStruct((2 * STAT_ROWS, query_count), jnp.float32)
    return pl.pallas_call(
        functools.partial(flash_kernel, parts, group_size, slots),
        in_specs=[pl.BlockSpec(memory_space=pltpu.SMEM), vmem, vmem, hbm, hbm, hbm],
        out_specs=[hbm] * (2 * len(parts) + 1) + [vmem],
        out_shape=halves + halves + [mass, stats],
        scratch_shapes=[
            pltpu.VMEM(queries.shape, jnp.bfloat16),
            pltpu.VMEM(keys.shape, jnp.bfloat16),
            pltpu.VMEM(values.shape, jnp.bfloat16),
            pltpu.VMEM((query_count, HD), jnp.float32),
            pltpu.VMEM((query_count, HD), jnp.float32),
            pltpu.VMEM((head_count // group_size, slots, tok_here, HD + width), jnp.bfloat16),
            pltpu.VMEM((2, query_count, HD), jnp.float32),
            pltpu.VMEM((head_count, 2, half, HD), jnp.float32),
            pltpu.VMEM(mass.shape, jnp.float32),
            pltpu.VMEM((query_count, HD), jnp.float32),
            pltpu.SemaphoreType.DMA((2 + head_count // group_size,)),
            pltpu.SemaphoreType.DMA((head_count, 2)),
            pltpu.SemaphoreType.DMA((groups,)),
        ],
        compiler_params=pltpu.CompilerParams(vmem_limit_bytes=FLASH_VMEM),
        cost_estimate=pl.CostEstimate(
            flops=work * 4 * HD, bytes_accessed=work, transcendentals=work
        ),
    )(lens, places, frequency, queries, keys, values)


def weigh_kernel(orders, head_counts, factor, own_ref, whole_ref, *refs):
    order_count = len(orders)
    tops_refs = refs[:order_count]
    mass_refs = refs[order_count : order_count + len(head_counts)]
    out_ref = refs[order_count + len(head_counts)]
    weight_refs = refs[order_count + len(head_counts) + 1 : -1]
    columns = refs[-1]
    me = lax.axis_index("ctx")
    top, inverse = whole_ref[:STAT_ROWS], 1.0 / whole_ref[STAT_ROWS:]
    mine = jnp.exp2(own_ref[:STAT_ROWS] - top) * inverse
    stretch_count = out_ref.shape[0]
    slots = max(1, HD // stretch_count)
    width = slots * stretch_count
    total, head = None, 0
    for count, mass_ref in zip(head_counts, mass_refs):
        for j in range(count):
            if j % slots == 0:
                turned = mass_ref[:, j // slots * width : (j // slots + 1) * width].T
            at = j % slots * stretch_count
            term = turned[at : at + stretch_count] * mine[head : head + 1]
            total = term if total is None else total + term
            head += 1
    out_ref[...] = total * factor
    theirs = [jnp.exp2(tops_ref[...] - top) * inverse for tops_ref in tops_refs]
    filled = (1 + order_count) * STAT_ROWS
    rest = jnp.zeros((HD - filled, top.shape[1]), jnp.float32)
    columns[...] = jnp.concatenate([mine] + theirs + [rest], axis=0).T
    for order, weight_ref in zip(orders, weight_refs):
        blocks = blocks_in_order(order)
        rows = columns.shape[0] // len(blocks)
        for place, rel in enumerate(blocks[: len(blocks) // 2]):
            source = pl.multiple_of((me ^ rel) * rows, rows)
            weight_ref[place * rows : (place + 1) * rows, :] = columns[pl.ds(source, rows), :]


def weigh(orders, head_counts, stretch_count, factor, own, whole, tops, masses):
    query_count = own.shape[1]
    vmem = pl.BlockSpec(memory_space=pltpu.VMEM)
    return pl.pallas_call(
        functools.partial(weigh_kernel, orders, head_counts, factor),
        in_specs=[vmem] * (2 + len(tops) + len(masses)),
        out_specs=[vmem] * (1 + len(orders)),
        out_shape=[jax.ShapeDtypeStruct((stretch_count, query_count), jnp.float32)]
        + [jax.ShapeDtypeStruct((query_count // 2, HD), jnp.float32)] * len(orders),
        scratch_shapes=[pltpu.VMEM((query_count, HD), jnp.float32)],
        compiler_params=pltpu.CompilerParams(vmem_limit_bytes=VMEM_LIMIT),
        cost_estimate=pl.CostEstimate(flops=1 << 20, bytes_accessed=1 << 20, transcendentals=1 << 14),
    )(own, whole, *tops, *masses)


def merge_kernel(first_head, other, keep_ref, got_ref, weight_ref, near_ref, far_ref):
    half = near_ref.shape[0]
    for j in range(keep_ref.shape[1] // HD):
        columns = slice(j * HD, (j + 1) * HD)
        head = first_head + j
        theirs = (1 + other) * STAT_ROWS + head
        for rows, target in ((slice(0, half), near_ref), (slice(half, 2 * half), far_ref)):
            target[:, columns] = (
                keep_ref[rows, columns] * weight_ref[rows, head : head + 1]
                + got_ref[rows, columns] * weight_ref[rows, theirs : theirs + 1]
            )


def merge(first_head, other, keep, got, weights):
    rows, columns = keep.shape
    vmem = pl.BlockSpec(memory_space=pltpu.VMEM)
    return pl.pallas_call(
        functools.partial(merge_kernel, first_head, other),
        in_specs=[vmem] * 3,
        out_specs=[vmem] * 2,
        out_shape=[jax.ShapeDtypeStruct((rows // 2, columns), jnp.float32)] * 2,
        compiler_params=pltpu.CompilerParams(vmem_limit_bytes=VMEM_LIMIT),
        cost_estimate=pl.CostEstimate(
            flops=3 * rows * columns, bytes_accessed=12 * rows * columns, transcendentals=0
        ),
    )(keep, got, weights)


def finish_kernel(count, *refs):
    mass_ref, mass_got_ref, attended_ref, out_ref = refs[2 * count :]
    at = 0
    for total_ref, got_ref in zip(refs[:count], refs[count : 2 * count]):
        columns = slice(at, at + total_ref.shape[1])
        attended_ref[:, columns] = (total_ref[...] + got_ref[...]).astype(attended_ref.dtype)
        at += total_ref.shape[1]
    out_ref[...] = mass_ref[...] + mass_got_ref[...]


def finish(totals, blocks, mass, mass_got):
    rows = totals[0].shape[0]
    columns = sum(total.shape[1] for total in totals)
    vmem = pl.BlockSpec(memory_space=pltpu.VMEM)
    return pl.pallas_call(
        functools.partial(finish_kernel, len(totals)),
        in_specs=[vmem] * (2 * len(totals) + 2),
        out_specs=[vmem] * 2,
        out_shape=[
            jax.ShapeDtypeStruct((rows, columns), jnp.bfloat16),
            jax.ShapeDtypeStruct(mass.shape, jnp.float32),
        ],
        compiler_params=pltpu.CompilerParams(vmem_limit_bytes=VMEM_LIMIT),
        cost_estimate=pl.CostEstimate(
            flops=rows * columns, bytes_accessed=10 * rows * columns, transcendentals=0
        ),
    )(*totals, *blocks, mass, mass_got)


def in_log2(stats):
    return jnp.concatenate([stats[:STAT_ROWS] * LOG2_SCALE, stats[STAT_ROWS:]], axis=0)


def join_stats(one, two):
    top = jnp.maximum(one[:STAT_ROWS], two[:STAT_ROWS])
    total = one[STAT_ROWS:] * jnp.exp2(one[:STAT_ROWS] - top) + two[STAT_ROWS:] * jnp.exp2(
        two[:STAT_ROWS] - top
    )
    return jnp.concatenate([top, total], axis=0)


def local(queries, keys, values, stretch_lengths, query_pos):
    query_count = queries.shape[0]
    heads_here = queries.shape[1] // HD
    group_size = heads_here // (keys.shape[1] // HD)
    stretch_count = stretch_lengths.shape[0]
    ctx_size, head_size = lax.axis_size("ctx"), lax.axis_size("head")
    bits = tuple(2**i for i in range(ctx_size.bit_length() - 1))
    head_bits = tuple(2**i for i in range(head_size.bit_length() - 1))
    results = {}

    def once(make):
        @functools.wraps(make)
        def cached(*key):
            if (make.__name__, *key) not in results:
                results[(make.__name__, *key)] = make(*key)
            return results[(make.__name__, *key)]

        return cached

    def exchange(array, axis, bit):
        return lax.ppermute(array, axis, [(i, i ^ bit) for i in range(lax.axis_size(axis))])

    def fenced(name, array, axis, bit):
        if (name,) not in FENCES:
            return exchange(array, axis, bit)
        return lax.cond(
            stretch_lengths[0] > 0, lambda sent: exchange(sent, axis, bit), jnp.zeros_like, array
        )

    def after(names, arrays):
        waits = [arrived(other) for name in names for other in TIES.get(name, ()) if known(other)]
        return lax.optimization_barrier((*arrays, *waits))[: len(arrays)] if waits else arrays

    def run(names, step, state):
        state = tuple(after(names, state))
        if len(names) == 1:
            return step(names[0], *state)

        def steps(*state):
            for name in names:
                state = step(name, *state)
            return state

        return lax.cond(stretch_lengths[0] > 0, steps, lambda *state: state, *state)

    def runs(names):
        fences = [tuple(name for name in fence if name in names) for fence in FENCES]
        fences = [fence for fence in fences if fence]
        fenced = {name for fence in fences for name in fence}
        starts = {fence[0]: fence for fence in fences}
        return [starts.get(name, (name,)) for name in names if name in starts or name not in fenced]

    lane = np.arange(HD) % (HD // 2)
    frequency = jnp.asarray((ROPE_BASE ** (-2.0 * lane / HD)).astype(np.float32).reshape(1, HD))
    places = query_pos.reshape(query_count // HD, HD)
    parts = []
    for count, turn in CHUNKS:
        rotated = bits[turn:] + bits[:turn]
        first = bits[-turn]
        moved = (first,) + tuple(bit for bit in bits if bit != first)
        parts.append((rotated if turn >= 0 else moved, count))
    parts = tuple(parts)
    mass_steps = ["h.%d" % bit for bit in head_bits] + ["m.%d" % bit for bit in bits]
    mass_steps.sort(key=lambda name: MASS_ORDER.index(name) if name in MASS_ORDER else len(MASS_ORDER))
    orders = {}
    for order, _ in parts:
        orders.setdefault(order, len(orders))
    *halves, masses, raw_stats = flash(
        parts, group_size, queries, keys, values, stretch_lengths, places, frequency
    )
    keeps, sends = halves[: len(parts)], halves[len(parts) :]
    own = lax.optimization_barrier(in_log2(raw_stats))
    firsts = [order[0] for order in orders]

    def known(name):
        kind, bit = name.split(".")
        if kind == "h":
            return int(bit) in head_bits
        return int(bit) in bits

    stat_steps = ["a.%d" % bit for bit in bits]
    stat_runs, mass_runs = runs(stat_steps), runs(mass_steps[:-1]) + [(mass_steps[-1],)]
    run_of = {name: i for names in (stat_runs, mass_runs) for i, run_ in enumerate(names) for name in run_}

    @once
    def arrived(name):
        kind, bit = name.split(".")
        if kind == "a":
            return stats(run_of[name] + 1)[0]
        if kind in ("h", "m"):
            return mass(run_of[name] + 1)[0]
        n, bit = int(kind[1:]), int(bit)
        i = parts[n][0].index(bit)
        send = sends[n] if i == 0 else halved(n, i)[1]
        return exchange(after([name], (send,))[0], "ctx", bit)

    def stat_step(name, joined, *tops):
        bit = int(name.split(".")[1])
        opening = bit == bits[0]
        message = raw_stats if opening else joined
        if bit in firsts and not opening:
            message = jnp.concatenate([message, own[:STAT_ROWS]], axis=0)
        got = fenced(name, message, "ctx", bit)
        joined = join_stats(joined, in_log2(got) if opening else got[: 2 * STAT_ROWS])
        if bit in firsts:
            top = got[:STAT_ROWS] * LOG2_SCALE if opening else got[2 * STAT_ROWS :]
            tops = tuple(top if i == firsts.index(bit) else old for i, old in enumerate(tops))
        return (joined, *tops)

    def mass_step(name, total):
        kind, bit = name.split(".")
        return (total + fenced(name, total, "head" if kind == "h" else "ctx", int(bit)),)

    @once
    def stats(step):
        if step == 0:
            return (own,) + (own[:STAT_ROWS],) * len(firsts)
        return run(stat_runs[step - 1], stat_step, stats(step - 1))

    @once
    def weighed():
        joined, *tops = stats(len(stat_runs))
        factor = stretch_count / (heads_here * head_size)
        return weigh(tuple(orders), (heads_here,), stretch_count, factor, own, joined, tops, [masses])

    @once
    def mass(step):
        if step == 0:
            return (weighed()[0],)
        return run(mass_runs[step - 1], mass_step, mass(step - 1))

    @once
    def halved(n, i):
        order, count = parts[n]
        got = arrived("c%d.%d" % (n, order[i - 1]))
        if i == 1:
            first_head = sum(c for _, c in parts[:n])
            kind = orders[order]
            return merge(first_head, kind, keeps[n], got, weighed()[1 + kind])
        total = halved(n, i - 1)[0] + got
        rows = total.shape[0] // 2
        return total[:rows], total[rows:]

    last = len(bits) - 1
    totals = [halved(n, last)[0] for n in range(len(parts))]
    blocks = [arrived("c%d.%d" % (n, order[last])) for n, (order, _) in enumerate(parts)]
    name = mass_steps[-1]
    (before,) = mass(len(mass_runs) - 1)
    got = exchange(after([name], (before,))[0], "head" if name[0] == "h" else "ctx", int(name[2:]))
    return tuple(finish(totals, blocks, before, got))


def solution(mesh):
    placed = (P(None, "head"), P("ctx", "head"), P("ctx", "head"), P(), P())
    return jax.shard_map(
        local, mesh=mesh, in_specs=placed, out_specs=(P("ctx", "head"), P()), check_vma=False
    )
```

```python
import functools
import math

import jax
import jax.numpy as jnp
import numpy as np
from jax import lax
from jax.experimental import pallas as pl
from jax.experimental.pallas import tpu as pltpu
from jax.sharding import PartitionSpec as P

HD = 128
ROPE_BASE = 1000000.0
LOG2_SCALE = HD ** (-0.5) * math.log2(math.e)
VMEM_LIMIT = 16 * 1024 * 1024
FLASH_VMEM = 60 * 1024 * 1024
STAT_ROWS = 16
TILE = 128
HALF_PI = (1.5706787109375, 1.1761486530303955e-4, 9.920935796805404e-10)

CHUNKS = ((4, 0), (4, 0), (2, 1))
TIES = {"c1.1": ("a.2",), "c2.2": ("a.2",), "h.1": ("c0.1",)}
FENCES = (("a.2",),)
MASS_ORDER = ("h.1", "h.2", "m.1", "m.4", "m.2")


def position(rel, order):
    place = 0
    for bit in order:
        place = place * 2 + ((rel // bit) & 1)
    return place


def blocks_in_order(order):
    return sorted(range(2 ** len(order)), key=lambda rel: position(rel, order))


def rope_tables(pos_ref, frequency_ref, cos_ref, sin_ref):
    query_count = cos_ref.shape[0]
    half = query_count // 2
    rows = []
    for group in range(query_count // HD):
        row = pos_ref[group : group + 1, :].astype(jnp.float32)
        rows.append(jnp.broadcast_to(row, (HD, HD)).T)
    places = jnp.concatenate(rows, axis=0)
    left = lax.broadcasted_iota(jnp.int32, (1, HD), 1) < HD // 2
    angle = jnp.where(left, places[:half], places[half:]) * frequency_ref[...]
    turns = jnp.floor(angle * (2.0 / math.pi) + 0.5)
    rest = ((angle - turns * HALF_PI[0]) - turns * HALF_PI[1]) - turns * HALF_PI[2]
    square = rest * rest
    sine = rest + rest * square * (
        -1.6666654611e-1 + square * (8.3321608736e-3 + square * -1.9515295891e-4)
    )
    cosine = (1.0 - 0.5 * square) + square * square * (
        4.166664568298827e-2 + square * (-1.388731625493765e-3 + square * 2.443315711809948e-5)
    )
    quarter = turns.astype(jnp.int32) & 3
    odd = (quarter & 1) == 1
    cos_value = jnp.where(odd, sine, cosine) * jnp.where((quarter == 1) | (quarter == 2), -1.0, 1.0)
    sin_value = jnp.where(odd, cosine, sine) * jnp.where(quarter >= 2, -1.0, 1.0)
    cos_other = pltpu.roll(cos_value, HD // 2, axis=1)
    sin_other = pltpu.roll(sin_value, HD // 2, axis=1)
    cos_ref[:half, :] = jnp.where(left, cos_value, cos_other)
    cos_ref[half:, :] = jnp.where(left, cos_other, cos_value)
    sin_ref[:half, :] = jnp.where(left, -sin_value, sin_other)
    sin_ref[half:, :] = jnp.where(left, -sin_other, sin_value)


def flash_kernel(parts, group_size, slots, lens_ref, pos_ref, frequency_ref, q_hbm, k_hbm, v_hbm, *refs):
    refs = list(refs)
    keeps = [refs.pop(0) for _ in parts]
    sends = [refs.pop(0) for _ in parts]
    mass_hbm, stats_ref = refs.pop(0), refs.pop(0)
    q_ref, k_ref, v_ref, cos_ref, sin_ref, values, whole, halves, mass_ref, columns = refs[:10]
    kv_sems, half_sems, mass_sems = refs[10:]
    query_count, tok_here = q_ref.shape[0], k_ref.shape[0]
    stretch_count = lens_ref.shape[0]
    me = lax.axis_index("ctx")
    head_count = sum(count for _, count in parts)
    kv_count = head_count // group_size
    width = slots * stretch_count

    k_copy = pltpu.make_async_copy(k_hbm, k_ref, kv_sems.at[0])
    v_copy = pltpu.make_async_copy(v_hbm, v_ref, kv_sems.at[1])
    k_copy.start()
    q_copies = []
    for g in range(kv_count):
        lanes = pl.ds(g * group_size * HD, group_size * HD)
        q_copies.append(
            pltpu.make_async_copy(q_hbm.at[:, lanes], q_ref.at[:, lanes], kv_sems.at[2 + g])
        )
    q_copies[0].start()
    v_copy.start()
    for copy in q_copies[1:]:
        copy.start()

    rope_tables(pos_ref, frequency_ref, cos_ref, sin_ref)
    lane = lax.broadcasted_iota(jnp.int32, columns.shape, 1)
    columns[...] = jnp.where(lane < STAT_ROWS, 0.0, 1.0)
    lane = lax.broadcasted_iota(jnp.int32, (1, width), 1)
    starts, ends = jnp.zeros((1, width), jnp.int32), jnp.zeros((1, width), jnp.int32)
    edge = -me * tok_here
    for c in range(stretch_count):
        here = (lane & (stretch_count - 1)) == c
        starts = jnp.where(here, edge, starts)
        edge = edge + lens_ref[c]
        ends = jnp.where(here, edge, ends)
    at = lax.broadcasted_iota(jnp.int32, (tok_here, width), 0)
    inside = jnp.where((at >= starts) & (at < ends), 1.0, 0.0)
    slot_of_lane = lane // stretch_count
    for slot in range(slots):
        marks = jnp.where(slot_of_lane == slot, inside, 0.0).astype(jnp.bfloat16)
        for g in range(kv_count):
            values[g, slot, :, HD:] = marks
    v_copy.wait()
    for g in range(kv_count):
        for slot in range(slots):
            values[g, slot, :, :HD] = v_ref[:, g * HD : (g + 1) * HD]
    k_copy.wait()
    for copy in q_copies:
        copy.wait()

    tile = min(TILE, query_count)
    half_copies, mass_copies = [], []
    for j in range(head_count):
        g = j // group_size
        lanes = slice(j // slots * width, (j // slots + 1) * width)
        for t in range(query_count // tile):
            rows = slice(t * tile, (t + 1) * tile)
            q = q_ref[rows, j * HD : (j + 1) * HD].astype(jnp.float32)
            turned = pltpu.roll(q, HD // 2, axis=1)
            roped = (q * cos_ref[rows, :] + turned * sin_ref[rows, :]).astype(jnp.bfloat16)
            raw = lax.dot_general(
                roped, k_ref[:, g * HD : (g + 1) * HD], (((1,), (1,)), ((), ())),
                preferred_element_type=jnp.float32,
            )
            top = jnp.max(raw, axis=1, keepdims=True)
            weights = jnp.exp2((raw - top) * LOG2_SCALE)
            columns[rows, j : j + 1] = top
            columns[rows, STAT_ROWS + j : STAT_ROWS + j + 1] = jnp.sum(weights, axis=1, keepdims=True)
            out = jnp.dot(
                weights.astype(jnp.bfloat16), values[g, j % slots], preferred_element_type=jnp.float32
            )
            whole[j % 2, rows, :] = out[:, :HD]
            if j % slots == 0:
                mass_ref[rows, lanes] = out[:, HD:]
            else:
                mass_ref[rows, lanes] += out[:, HD:]
        part, local_head = 0, j
        while local_head >= parts[part][1]:
            local_head -= parts[part][1]
            part += 1
        blocks = blocks_in_order(parts[part][0])
        size = query_count // len(blocks)
        half = len(blocks) // 2
        for place, rel in enumerate(blocks):
            source = pl.multiple_of((me ^ rel) * size, size)
            side, place = place // half, place % half
            halves[j, side, place * size : (place + 1) * size, :] = whole[j % 2, pl.ds(source, size), :]
        if local_head == parts[part][1] - 1:
            first_head = j - local_head
            for i in range(first_head, j + 1):
                lanes = pl.ds((i - first_head) * HD, HD)
                for side, target in ((0, keeps[part]), (1, sends[part])):
                    half_copies.append(
                        pltpu.make_async_copy(
                            halves.at[i, side], target.at[:, lanes], half_sems.at[i, side]
                        )
                    )
                    half_copies[-1].start()
            whole_groups = (j + 1) // slots if j < head_count - 1 else -(-head_count // slots)
            for group in range(len(mass_copies), whole_groups):
                lanes = pl.ds(group * width, width)
                mass_copies.append(
                    pltpu.make_async_copy(
                        mass_ref.at[:, lanes], mass_hbm.at[:, lanes], mass_sems.at[group]
                    )
                )
                mass_copies[-1].start()
    stats_ref[...] = columns[...].T[: 2 * STAT_ROWS]
    for copy in half_copies + mass_copies:
        copy.wait()


def flash(parts, group_size, queries, keys, values, lens, places, frequency):
    query_count = queries.shape[0]
    tok_here = keys.shape[0]
    stretch_count = lens.shape[0]
    head_count = sum(count for _, count in parts)
    half = query_count // 2
    slots = max(1, HD // stretch_count)
    width = slots * stretch_count
    groups = -(-head_count // slots)
    work = head_count * query_count * tok_here
    vmem = pl.BlockSpec(memory_space=pltpu.VMEM)
    hbm = pl.BlockSpec(memory_space=pltpu.HBM)
    halves = [jax.ShapeDtypeStruct((half, count * HD), jnp.float32) for _, count in parts]
    mass = jax.ShapeDtypeStruct((query_count, groups * width), jnp.float32)
    stats = jax.ShapeDtypeStruct((2 * STAT_ROWS, query_count), jnp.float32)
    return pl.pallas_call(
        functools.partial(flash_kernel, parts, group_size, slots),
        in_specs=[pl.BlockSpec(memory_space=pltpu.SMEM), vmem, vmem, hbm, hbm, hbm],
        out_specs=[hbm] * (2 * len(parts) + 1) + [vmem],
        out_shape=halves + halves + [mass, stats],
        scratch_shapes=[
            pltpu.VMEM(queries.shape, jnp.bfloat16),
            pltpu.VMEM(keys.shape, jnp.bfloat16),
            pltpu.VMEM(values.shape, jnp.bfloat16),
            pltpu.VMEM((query_count, HD), jnp.float32),
            pltpu.VMEM((query_count, HD), jnp.float32),
            pltpu.VMEM((head_count // group_size, slots, tok_here, HD + width), jnp.bfloat16),
            pltpu.VMEM((2, query_count, HD), jnp.float32),
            pltpu.VMEM((head_count, 2, half, HD), jnp.float32),
            pltpu.VMEM(mass.shape, jnp.float32),
            pltpu.VMEM((query_count, HD), jnp.float32),
            pltpu.SemaphoreType.DMA((2 + head_count // group_size,)),
            pltpu.SemaphoreType.DMA((head_count, 2)),
            pltpu.SemaphoreType.DMA((groups,)),
        ],
        compiler_params=pltpu.CompilerParams(vmem_limit_bytes=FLASH_VMEM),
        cost_estimate=pl.CostEstimate(
            flops=work * 4 * HD, bytes_accessed=work, transcendentals=work
        ),
    )(lens, places, frequency, queries, keys, values)


def weigh_kernel(orders, head_counts, factor, own_ref, whole_ref, *refs):
    order_count = len(orders)
    tops_refs = refs[:order_count]
    mass_refs = refs[order_count : order_count + len(head_counts)]
    out_ref = refs[order_count + len(head_counts)]
    weight_refs = refs[order_count + len(head_counts) + 1 : -1]
    columns = refs[-1]
    me = lax.axis_index("ctx")
    top, inverse = whole_ref[:STAT_ROWS], 1.0 / whole_ref[STAT_ROWS:]
    mine = jnp.exp2(own_ref[:STAT_ROWS] - top) * inverse
    stretch_count = out_ref.shape[0]
    slots = max(1, HD // stretch_count)
    width = slots * stretch_count
    total, head = None, 0
    for count, mass_ref in zip(head_counts, mass_refs):
        for j in range(count):
            if j % slots == 0:
                turned = mass_ref[:, j // slots * width : (j // slots + 1) * width].T
            at = j % slots * stretch_count
            term = turned[at : at + stretch_count] * mine[head : head + 1]
            total = term if total is None else total + term
            head += 1
    out_ref[...] = total * factor
    theirs = [jnp.exp2(tops_ref[...] - top) * inverse for tops_ref in tops_refs]
    filled = (1 + order_count) * STAT_ROWS
    rest = jnp.zeros((HD - filled, top.shape[1]), jnp.float32)
    columns[...] = jnp.concatenate([mine] + theirs + [rest], axis=0).T
    for order, weight_ref in zip(orders, weight_refs):
        blocks = blocks_in_order(order)
        rows = columns.shape[0] // len(blocks)
        for place, rel in enumerate(blocks[: len(blocks) // 2]):
            source = pl.multiple_of((me ^ rel) * rows, rows)
            weight_ref[place * rows : (place + 1) * rows, :] = columns[pl.ds(source, rows), :]


def weigh(orders, head_counts, stretch_count, factor, own, whole, tops, masses):
    query_count = own.shape[1]
    vmem = pl.BlockSpec(memory_space=pltpu.VMEM)
    return pl.pallas_call(
        functools.partial(weigh_kernel, orders, head_counts, factor),
        in_specs=[vmem] * (2 + len(tops) + len(masses)),
        out_specs=[vmem] * (1 + len(orders)),
        out_shape=[jax.ShapeDtypeStruct((stretch_count, query_count), jnp.float32)]
        + [jax.ShapeDtypeStruct((query_count // 2, HD), jnp.float32)] * len(orders),
        scratch_shapes=[pltpu.VMEM((query_count, HD), jnp.float32)],
        compiler_params=pltpu.CompilerParams(vmem_limit_bytes=VMEM_LIMIT),
        cost_estimate=pl.CostEstimate(flops=1 << 20, bytes_accessed=1 << 20, transcendentals=1 << 14),
    )(own, whole, *tops, *masses)


def merge_kernel(first_head, other, keep_ref, got_ref, weight_ref, near_ref, far_ref):
    half = near_ref.shape[0]
    for j in range(keep_ref.shape[1] // HD):
        columns = slice(j * HD, (j + 1) * HD)
        head = first_head + j
        theirs = (1 + other) * STAT_ROWS + head
        for rows, target in ((slice(0, half), near_ref), (slice(half, 2 * half), far_ref)):
            target[:, columns] = (
                keep_ref[rows, columns] * weight_ref[rows, head : head + 1]
                + got_ref[rows, columns] * weight_ref[rows, theirs : theirs + 1]
            )


def merge(first_head, other, keep, got, weights):
    rows, columns = keep.shape
    vmem = pl.BlockSpec(memory_space=pltpu.VMEM)
    return pl.pallas_call(
        functools.partial(merge_kernel, first_head, other),
        in_specs=[vmem] * 3,
        out_specs=[vmem] * 2,
        out_shape=[jax.ShapeDtypeStruct((rows // 2, columns), jnp.float32)] * 2,
        compiler_params=pltpu.CompilerParams(vmem_limit_bytes=VMEM_LIMIT),
        cost_estimate=pl.CostEstimate(
            flops=3 * rows * columns, bytes_accessed=12 * rows * columns, transcendentals=0
        ),
    )(keep, got, weights)


def finish_kernel(count, *refs):
    mass_ref, mass_got_ref, attended_ref, out_ref = refs[2 * count :]
    at = 0
    for total_ref, got_ref in zip(refs[:count], refs[count : 2 * count]):
        columns = slice(at, at + total_ref.shape[1])
        attended_ref[:, columns] = (total_ref[...] + got_ref[...]).astype(attended_ref.dtype)
        at += total_ref.shape[1]
    out_ref[...] = mass_ref[...] + mass_got_ref[...]


def finish(totals, blocks, mass, mass_got):
    rows = totals[0].shape[0]
    columns = sum(total.shape[1] for total in totals)
    vmem = pl.BlockSpec(memory_space=pltpu.VMEM)
    return pl.pallas_call(
        functools.partial(finish_kernel, len(totals)),
        in_specs=[vmem] * (2 * len(totals) + 2),
        out_specs=[vmem] * 2,
        out_shape=[
            jax.ShapeDtypeStruct((rows, columns), jnp.bfloat16),
            jax.ShapeDtypeStruct(mass.shape, jnp.float32),
        ],
        compiler_params=pltpu.CompilerParams(vmem_limit_bytes=VMEM_LIMIT),
        cost_estimate=pl.CostEstimate(
            flops=rows * columns, bytes_accessed=10 * rows * columns, transcendentals=0
        ),
    )(*totals, *blocks, mass, mass_got)


def in_log2(stats):
    return jnp.concatenate([stats[:STAT_ROWS] * LOG2_SCALE, stats[STAT_ROWS:]], axis=0)


def join_stats(one, two):
    top = jnp.maximum(one[:STAT_ROWS], two[:STAT_ROWS])
    total = one[STAT_ROWS:] * jnp.exp2(one[:STAT_ROWS] - top) + two[STAT_ROWS:] * jnp.exp2(
        two[:STAT_ROWS] - top
    )
    return jnp.concatenate([top, total], axis=0)


def local(queries, keys, values, stretch_lengths, query_pos):
    query_count = queries.shape[0]
    heads_here = queries.shape[1] // HD
    group_size = heads_here // (keys.shape[1] // HD)
    stretch_count = stretch_lengths.shape[0]
    ctx_size, head_size = lax.axis_size("ctx"), lax.axis_size("head")
    bits = tuple(2**i for i in range(ctx_size.bit_length() - 1))
    head_bits = tuple(2**i for i in range(head_size.bit_length() - 1))
    results = {}

    def once(make):
        @functools.wraps(make)
        def cached(*key):
            if (make.__name__, *key) not in results:
                results[(make.__name__, *key)] = make(*key)
            return results[(make.__name__, *key)]

        return cached

    def exchange(array, axis, bit):
        return lax.ppermute(array, axis, [(i, i ^ bit) for i in range(lax.axis_size(axis))])

    def fenced(name, array, axis, bit):
        if (name,) not in FENCES:
            return exchange(array, axis, bit)
        return lax.cond(
            stretch_lengths[0] > 0, lambda sent: exchange(sent, axis, bit), jnp.zeros_like, array
        )

    def after(names, arrays):
        waits = [arrived(other) for name in names for other in TIES.get(name, ()) if known(other)]
        return lax.optimization_barrier((*arrays, *waits))[: len(arrays)] if waits else arrays

    def run(names, step, state):
        state = tuple(after(names, state))
        if len(names) == 1:
            return step(names[0], *state)

        def steps(*state):
            for name in names:
                state = step(name, *state)
            return state

        return lax.cond(stretch_lengths[0] > 0, steps, lambda *state: state, *state)

    def runs(names):
        fences = [tuple(name for name in fence if name in names) for fence in FENCES]
        fences = [fence for fence in fences if fence]
        fenced = {name for fence in fences for name in fence}
        starts = {fence[0]: fence for fence in fences}
        return [starts.get(name, (name,)) for name in names if name in starts or name not in fenced]

    lane = np.arange(HD) % (HD // 2)
    frequency = jnp.asarray((ROPE_BASE ** (-2.0 * lane / HD)).astype(np.float32).reshape(1, HD))
    places = query_pos.reshape(query_count // HD, HD)
    parts = []
    for count, turn in CHUNKS:
        rotated = bits[turn:] + bits[:turn]
        first = bits[-turn]
        moved = (first,) + tuple(bit for bit in bits if bit != first)
        parts.append((rotated if turn >= 0 else moved, count))
    parts = tuple(parts)
    mass_steps = ["h.%d" % bit for bit in head_bits] + ["m.%d" % bit for bit in bits]
    mass_steps.sort(key=lambda name: MASS_ORDER.index(name) if name in MASS_ORDER else len(MASS_ORDER))
    orders = {}
    for order, _ in parts:
        orders.setdefault(order, len(orders))
    *halves, masses, raw_stats = flash(
        parts, group_size, queries, keys, values, stretch_lengths, places, frequency
    )
    keeps, sends = halves[: len(parts)], halves[len(parts) :]
    own = lax.optimization_barrier(in_log2(raw_stats))
    firsts = [order[0] for order in orders]

    def known(name):
        kind, bit = name.split(".")
        if kind == "h":
            return int(bit) in head_bits
        return int(bit) in bits

    stat_steps = ["a.%d" % bit for bit in bits]
    stat_runs, mass_runs = runs(stat_steps), runs(mass_steps[:-1]) + [(mass_steps[-1],)]
    run_of = {name: i for names in (stat_runs, mass_runs) for i, run_ in enumerate(names) for name in run_}

    @once
    def arrived(name):
        kind, bit = name.split(".")
        if kind == "a":
            return stats(run_of[name] + 1)[0]
        if kind in ("h", "m"):
            return mass(run_of[name] + 1)[0]
        n, bit = int(kind[1:]), int(bit)
        i = parts[n][0].index(bit)
        send = sends[n] if i == 0 else halved(n, i)[1]
        return exchange(after([name], (send,))[0], "ctx", bit)

    def stat_step(name, joined, *tops):
        bit = int(name.split(".")[1])
        opening = bit == bits[0]
        message = raw_stats if opening else joined
        if bit in firsts and not opening:
            message = jnp.concatenate([message, own[:STAT_ROWS]], axis=0)
        got = fenced(name, message, "ctx", bit)
        joined = join_stats(joined, in_log2(got) if opening else got[: 2 * STAT_ROWS])
        if bit in firsts:
            top = got[:STAT_ROWS] * LOG2_SCALE if opening else got[2 * STAT_ROWS :]
            tops = tuple(top if i == firsts.index(bit) else old for i, old in enumerate(tops))
        return (joined, *tops)

    def mass_step(name, total):
        kind, bit = name.split(".")
        return (total + fenced(name, total, "head" if kind == "h" else "ctx", int(bit)),)

    @once
    def stats(step):
        if step == 0:
            return (own,) + (own[:STAT_ROWS],) * len(firsts)
        return run(stat_runs[step - 1], stat_step, stats(step - 1))

    @once
    def weighed():
        joined, *tops = stats(len(stat_runs))
        factor = stretch_count / (heads_here * head_size)
        return weigh(tuple(orders), (heads_here,), stretch_count, factor, own, joined, tops, [masses])

    @once
    def mass(step):
        if step == 0:
            return (weighed()[0],)
        return run(mass_runs[step - 1], mass_step, mass(step - 1))

    @once
    def halved(n, i):
        order, count = parts[n]
        got = arrived("c%d.%d" % (n, order[i - 1]))
        if i == 1:
            first_head = sum(c for _, c in parts[:n])
            kind = orders[order]
            return merge(first_head, kind, keeps[n], got, weighed()[1 + kind])
        total = halved(n, i - 1)[0] + got
        rows = total.shape[0] // 2
        return total[:rows], total[rows:]

    last = len(bits) - 1
    totals = [halved(n, last)[0] for n in range(len(parts))]
    blocks = [arrived("c%d.%d" % (n, order[last])) for n, (order, _) in enumerate(parts)]
    name = mass_steps[-1]
    (before,) = mass(len(mass_runs) - 1)
    got = exchange(after([name], (before,))[0], "head" if name[0] == "h" else "ctx", int(name[2:]))
    return tuple(finish(totals, blocks, before, got))


def solution(mesh):
    placed = (P(None, "head"), P("ctx", "head"), P("ctx", "head"), P(), P())
    return jax.shard_map(
        local, mesh=mesh, in_specs=placed, out_specs=(P("ctx", "head"), P()), check_vma=False
    )
```

```python
import functools
import math

import jax
import jax.numpy as jnp
import numpy as np
from jax import lax
from jax.experimental import pallas as pl
from jax.experimental.pallas import tpu as pltpu
from jax.sharding import PartitionSpec as P

HD = 128
ROPE_BASE = 1000000.0
LOG2_SCALE = HD ** (-0.5) * math.log2(math.e)
VMEM_LIMIT = 16 * 1024 * 1024
FLASH_VMEM = 60 * 1024 * 1024
STAT_ROWS = 16
TILE = 128
HALF_PI = (1.5706787109375, 1.1761486530303955e-4, 9.920935796805404e-10)

CHUNKS = ((4, 0), (4, 0), (2, 1))
TIES = {"h.1": ("c0.1",)}
FENCES = (("a.2",),)
MASS_ORDER = ("h.1", "h.2", "m.1", "m.4", "m.2")


def position(rel, order):
    place = 0
    for bit in order:
        place = place * 2 + ((rel // bit) & 1)
    return place


def blocks_in_order(order):
    return sorted(range(2 ** len(order)), key=lambda rel: position(rel, order))


def rope_tables(pos_ref, frequency_ref, cos_ref, sin_ref):
    query_count = cos_ref.shape[0]
    half = query_count // 2
    rows = []
    for group in range(query_count // HD):
        row = pos_ref[group : group + 1, :].astype(jnp.float32)
        rows.append(jnp.broadcast_to(row, (HD, HD)).T)
    places = jnp.concatenate(rows, axis=0)
    left = lax.broadcasted_iota(jnp.int32, (1, HD), 1) < HD // 2
    angle = jnp.where(left, places[:half], places[half:]) * frequency_ref[...]
    turns = jnp.floor(angle * (2.0 / math.pi) + 0.5)
    rest = ((angle - turns * HALF_PI[0]) - turns * HALF_PI[1]) - turns * HALF_PI[2]
    square = rest * rest
    sine = rest + rest * square * (
        -1.6666654611e-1 + square * (8.3321608736e-3 + square * -1.9515295891e-4)
    )
    cosine = (1.0 - 0.5 * square) + square * square * (
        4.166664568298827e-2 + square * (-1.388731625493765e-3 + square * 2.443315711809948e-5)
    )
    quarter = turns.astype(jnp.int32) & 3
    odd = (quarter & 1) == 1
    cos_value = jnp.where(odd, sine, cosine) * jnp.where((quarter == 1) | (quarter == 2), -1.0, 1.0)
    sin_value = jnp.where(odd, cosine, sine) * jnp.where(quarter >= 2, -1.0, 1.0)
    cos_other = pltpu.roll(cos_value, HD // 2, axis=1)
    sin_other = pltpu.roll(sin_value, HD // 2, axis=1)
    cos_ref[:half, :] = jnp.where(left, cos_value, cos_other)
    cos_ref[half:, :] = jnp.where(left, cos_other, cos_value)
    sin_ref[:half, :] = jnp.where(left, -sin_value, sin_other)
    sin_ref[half:, :] = jnp.where(left, -sin_other, sin_value)


def flash_kernel(parts, group_size, slots, lens_ref, pos_ref, frequency_ref, q_hbm, k_hbm, v_hbm, *refs):
    refs = list(refs)
    keeps = [refs.pop(0) for _ in parts]
    sends = [refs.pop(0) for _ in parts]
    mass_hbm, stats_ref = refs.pop(0), refs.pop(0)
    q_ref, k_ref, v_ref, cos_ref, sin_ref, values, whole, halves, mass_ref, columns = refs[:10]
    kv_sems, half_sems, mass_sems = refs[10:]
    query_count, tok_here = q_ref.shape[0], k_ref.shape[0]
    stretch_count = lens_ref.shape[0]
    me = lax.axis_index("ctx")
    head_count = sum(count for _, count in parts)
    kv_count = head_count // group_size
    width = slots * stretch_count

    k_copy = pltpu.make_async_copy(k_hbm, k_ref, kv_sems.at[0])
    v_copy = pltpu.make_async_copy(v_hbm, v_ref, kv_sems.at[1])
    k_copy.start()
    q_copies = []
    for g in range(kv_count):
        lanes = pl.ds(g * group_size * HD, group_size * HD)
        q_copies.append(
            pltpu.make_async_copy(q_hbm.at[:, lanes], q_ref.at[:, lanes], kv_sems.at[2 + g])
        )
    q_copies[0].start()
    v_copy.start()
    for copy in q_copies[1:]:
        copy.start()

    rope_tables(pos_ref, frequency_ref, cos_ref, sin_ref)
    lane = lax.broadcasted_iota(jnp.int32, columns.shape, 1)
    columns[...] = jnp.where(lane < STAT_ROWS, 0.0, 1.0)
    lane = lax.broadcasted_iota(jnp.int32, (1, width), 1)
    starts, ends = jnp.zeros((1, width), jnp.int32), jnp.zeros((1, width), jnp.int32)
    edge = -me * tok_here
    for c in range(stretch_count):
        here = (lane & (stretch_count - 1)) == c
        starts = jnp.where(here, edge, starts)
        edge = edge + lens_ref[c]
        ends = jnp.where(here, edge, ends)
    at = lax.broadcasted_iota(jnp.int32, (tok_here, width), 0)
    inside = jnp.where((at >= starts) & (at < ends), 1.0, 0.0)
    slot_of_lane = lane // stretch_count
    for slot in range(slots):
        marks = jnp.where(slot_of_lane == slot, inside, 0.0).astype(jnp.bfloat16)
        for g in range(kv_count):
            values[g, slot, :, HD:] = marks
    v_copy.wait()
    for g in range(kv_count):
        for slot in range(slots):
            values[g, slot, :, :HD] = v_ref[:, g * HD : (g + 1) * HD]
    k_copy.wait()
    for copy in q_copies:
        copy.wait()

    tile = min(TILE, query_count)
    half_copies, mass_copies = [], []
    for j in range(head_count):
        g = j // group_size
        lanes = slice(j // slots * width, (j // slots + 1) * width)
        for t in range(query_count // tile):
            rows = slice(t * tile, (t + 1) * tile)
            q = q_ref[rows, j * HD : (j + 1) * HD].astype(jnp.float32)
            turned = pltpu.roll(q, HD // 2, axis=1)
            roped = (q * cos_ref[rows, :] + turned * sin_ref[rows, :]).astype(jnp.bfloat16)
            raw = lax.dot_general(
                roped, k_ref[:, g * HD : (g + 1) * HD], (((1,), (1,)), ((), ())),
                preferred_element_type=jnp.float32,
            )
            top = jnp.max(raw, axis=1, keepdims=True)
            weights = jnp.exp2((raw - top) * LOG2_SCALE)
            columns[rows, j : j + 1] = top
            columns[rows, STAT_ROWS + j : STAT_ROWS + j + 1] = jnp.sum(weights, axis=1, keepdims=True)
            out = jnp.dot(
                weights.astype(jnp.bfloat16), values[g, j % slots], preferred_element_type=jnp.float32
            )
            whole[j % 2, rows, :] = out[:, :HD]
            if j % slots == 0:
                mass_ref[rows, lanes] = out[:, HD:]
            else:
                mass_ref[rows, lanes] += out[:, HD:]
        part, local_head = 0, j
        while local_head >= parts[part][1]:
            local_head -= parts[part][1]
            part += 1
        blocks = blocks_in_order(parts[part][0])
        size = query_count // len(blocks)
        half = len(blocks) // 2
        for place, rel in enumerate(blocks):
            source = pl.multiple_of((me ^ rel) * size, size)
            side, place = place // half, place % half
            halves[j, side, place * size : (place + 1) * size, :] = whole[j % 2, pl.ds(source, size), :]
        if local_head == parts[part][1] - 1:
            first_head = j - local_head
            for i in range(first_head, j + 1):
                lanes = pl.ds((i - first_head) * HD, HD)
                for side, target in ((0, keeps[part]), (1, sends[part])):
                    half_copies.append(
                        pltpu.make_async_copy(
                            halves.at[i, side], target.at[:, lanes], half_sems.at[i, side]
                        )
                    )
                    half_copies[-1].start()
            whole_groups = (j + 1) // slots if j < head_count - 1 else -(-head_count // slots)
            for group in range(len(mass_copies), whole_groups):
                lanes = pl.ds(group * width, width)
                mass_copies.append(
                    pltpu.make_async_copy(
                        mass_ref.at[:, lanes], mass_hbm.at[:, lanes], mass_sems.at[group]
                    )
                )
                mass_copies[-1].start()
    stats_ref[...] = columns[...].T[: 2 * STAT_ROWS]
    for copy in half_copies + mass_copies:
        copy.wait()


def flash(parts, group_size, queries, keys, values, lens, places, frequency):
    query_count = queries.shape[0]
    tok_here = keys.shape[0]
    stretch_count = lens.shape[0]
    head_count = sum(count for _, count in parts)
    half = query_count // 2
    slots = max(1, HD // stretch_count)
    width = slots * stretch_count
    groups = -(-head_count // slots)
    work = head_count * query_count * tok_here
    vmem = pl.BlockSpec(memory_space=pltpu.VMEM)
    hbm = pl.BlockSpec(memory_space=pltpu.HBM)
    halves = [jax.ShapeDtypeStruct((half, count * HD), jnp.float32) for _, count in parts]
    mass = jax.ShapeDtypeStruct((query_count, groups * width), jnp.float32)
    stats = jax.ShapeDtypeStruct((2 * STAT_ROWS, query_count), jnp.float32)
    return pl.pallas_call(
        functools.partial(flash_kernel, parts, group_size, slots),
        in_specs=[pl.BlockSpec(memory_space=pltpu.SMEM), vmem, vmem, hbm, hbm, hbm],
        out_specs=[hbm] * (2 * len(parts) + 1) + [vmem],
        out_shape=halves + halves + [mass, stats],
        scratch_shapes=[
            pltpu.VMEM(queries.shape, jnp.bfloat16),
            pltpu.VMEM(keys.shape, jnp.bfloat16),
            pltpu.VMEM(values.shape, jnp.bfloat16),
            pltpu.VMEM((query_count, HD), jnp.float32),
            pltpu.VMEM((query_count, HD), jnp.float32),
            pltpu.VMEM((head_count // group_size, slots, tok_here, HD + width), jnp.bfloat16),
            pltpu.VMEM((2, query_count, HD), jnp.float32),
            pltpu.VMEM((head_count, 2, half, HD), jnp.float32),
            pltpu.VMEM(mass.shape, jnp.float32),
            pltpu.VMEM((query_count, HD), jnp.float32),
            pltpu.SemaphoreType.DMA((2 + head_count // group_size,)),
            pltpu.SemaphoreType.DMA((head_count, 2)),
            pltpu.SemaphoreType.DMA((groups,)),
        ],
        compiler_params=pltpu.CompilerParams(vmem_limit_bytes=FLASH_VMEM),
        cost_estimate=pl.CostEstimate(
            flops=work * 4 * HD, bytes_accessed=work, transcendentals=work
        ),
    )(lens, places, frequency, queries, keys, values)


def weigh_kernel(orders, head_counts, factor, own_ref, whole_ref, *refs):
    order_count = len(orders)
    tops_refs = refs[:order_count]
    mass_refs = refs[order_count : order_count + len(head_counts)]
    out_ref = refs[order_count + len(head_counts)]
    weight_refs = refs[order_count + len(head_counts) + 1 : -1]
    columns = refs[-1]
    me = lax.axis_index("ctx")
    top, inverse = whole_ref[:STAT_ROWS], 1.0 / whole_ref[STAT_ROWS:]
    mine = jnp.exp2(own_ref[:STAT_ROWS] - top) * inverse
    stretch_count = out_ref.shape[0]
    slots = max(1, HD // stretch_count)
    width = slots * stretch_count
    total, head = None, 0
    for count, mass_ref in zip(head_counts, mass_refs):
        for j in range(count):
            if j % slots == 0:
                turned = mass_ref[:, j // slots * width : (j // slots + 1) * width].T
            at = j % slots * stretch_count
            term = turned[at : at + stretch_count] * mine[head : head + 1]
            total = term if total is None else total + term
            head += 1
    out_ref[...] = total * factor
    theirs = [jnp.exp2(tops_ref[...] - top) * inverse for tops_ref in tops_refs]
    filled = (1 + order_count) * STAT_ROWS
    rest = jnp.zeros((HD - filled, top.shape[1]), jnp.float32)
    columns[...] = jnp.concatenate([mine] + theirs + [rest], axis=0).T
    for order, weight_ref in zip(orders, weight_refs):
        blocks = blocks_in_order(order)
        rows = columns.shape[0] // len(blocks)
        for place, rel in enumerate(blocks[: len(blocks) // 2]):
            source = pl.multiple_of((me ^ rel) * rows, rows)
            weight_ref[place * rows : (place + 1) * rows, :] = columns[pl.ds(source, rows), :]


def weigh(orders, head_counts, stretch_count, factor, own, whole, tops, masses):
    query_count = own.shape[1]
    vmem = pl.BlockSpec(memory_space=pltpu.VMEM)
    return pl.pallas_call(
        functools.partial(weigh_kernel, orders, head_counts, factor),
        in_specs=[vmem] * (2 + len(tops) + len(masses)),
        out_specs=[vmem] * (1 + len(orders)),
        out_shape=[jax.ShapeDtypeStruct((stretch_count, query_count), jnp.float32)]
        + [jax.ShapeDtypeStruct((query_count // 2, HD), jnp.float32)] * len(orders),
        scratch_shapes=[pltpu.VMEM((query_count, HD), jnp.float32)],
        compiler_params=pltpu.CompilerParams(vmem_limit_bytes=VMEM_LIMIT),
        cost_estimate=pl.CostEstimate(flops=1 << 20, bytes_accessed=1 << 20, transcendentals=1 << 14),
    )(own, whole, *tops, *masses)


def merge_kernel(first_head, other, keep_ref, got_ref, weight_ref, near_ref, far_ref):
    half = near_ref.shape[0]
    for j in range(keep_ref.shape[1] // HD):
        columns = slice(j * HD, (j + 1) * HD)
        head = first_head + j
        theirs = (1 + other) * STAT_ROWS + head
        for rows, target in ((slice(0, half), near_ref), (slice(half, 2 * half), far_ref)):
            target[:, columns] = (
                keep_ref[rows, columns] * weight_ref[rows, head : head + 1]
                + got_ref[rows, columns] * weight_ref[rows, theirs : theirs + 1]
            )


def merge(first_head, other, keep, got, weights):
    rows, columns = keep.shape
    vmem = pl.BlockSpec(memory_space=pltpu.VMEM)
    return pl.pallas_call(
        functools.partial(merge_kernel, first_head, other),
        in_specs=[vmem] * 3,
        out_specs=[vmem] * 2,
        out_shape=[jax.ShapeDtypeStruct((rows // 2, columns), jnp.float32)] * 2,
        compiler_params=pltpu.CompilerParams(vmem_limit_bytes=VMEM_LIMIT),
        cost_estimate=pl.CostEstimate(
            flops=3 * rows * columns, bytes_accessed=12 * rows * columns, transcendentals=0
        ),
    )(keep, got, weights)


def finish_kernel(count, *refs):
    mass_ref, mass_got_ref, attended_ref, out_ref = refs[2 * count :]
    at = 0
    for total_ref, got_ref in zip(refs[:count], refs[count : 2 * count]):
        columns = slice(at, at + total_ref.shape[1])
        attended_ref[:, columns] = (total_ref[...] + got_ref[...]).astype(attended_ref.dtype)
        at += total_ref.shape[1]
    out_ref[...] = mass_ref[...] + mass_got_ref[...]


def finish(totals, blocks, mass, mass_got):
    rows = totals[0].shape[0]
    columns = sum(total.shape[1] for total in totals)
    vmem = pl.BlockSpec(memory_space=pltpu.VMEM)
    return pl.pallas_call(
        functools.partial(finish_kernel, len(totals)),
        in_specs=[vmem] * (2 * len(totals) + 2),
        out_specs=[vmem] * 2,
        out_shape=[
            jax.ShapeDtypeStruct((rows, columns), jnp.bfloat16),
            jax.ShapeDtypeStruct(mass.shape, jnp.float32),
        ],
        compiler_params=pltpu.CompilerParams(vmem_limit_bytes=VMEM_LIMIT),
        cost_estimate=pl.CostEstimate(
            flops=rows * columns, bytes_accessed=10 * rows * columns, transcendentals=0
        ),
    )(*totals, *blocks, mass, mass_got)


def in_log2(stats):
    return jnp.concatenate([stats[:STAT_ROWS] * LOG2_SCALE, stats[STAT_ROWS:]], axis=0)


def join_stats(one, two):
    top = jnp.maximum(one[:STAT_ROWS], two[:STAT_ROWS])
    total = one[STAT_ROWS:] * jnp.exp2(one[:STAT_ROWS] - top) + two[STAT_ROWS:] * jnp.exp2(
        two[:STAT_ROWS] - top
    )
    return jnp.concatenate([top, total], axis=0)


def local(queries, keys, values, stretch_lengths, query_pos):
    query_count = queries.shape[0]
    heads_here = queries.shape[1] // HD
    group_size = heads_here // (keys.shape[1] // HD)
    stretch_count = stretch_lengths.shape[0]
    ctx_size, head_size = lax.axis_size("ctx"), lax.axis_size("head")
    bits = tuple(2**i for i in range(ctx_size.bit_length() - 1))
    head_bits = tuple(2**i for i in range(head_size.bit_length() - 1))
    results = {}

    def once(make):
        @functools.wraps(make)
        def cached(*key):
            if (make.__name__, *key) not in results:
                results[(make.__name__, *key)] = make(*key)
            return results[(make.__name__, *key)]

        return cached

    def exchange(array, axis, bit):
        return lax.ppermute(array, axis, [(i, i ^ bit) for i in range(lax.axis_size(axis))])

    def fenced(name, array, axis, bit):
        if (name,) not in FENCES:
            return exchange(array, axis, bit)
        return lax.cond(
            stretch_lengths[0] > 0, lambda sent: exchange(sent, axis, bit), jnp.zeros_like, array
        )

    def after(names, arrays):
        waits = [arrived(other) for name in names for other in TIES.get(name, ()) if known(other)]
        return lax.optimization_barrier((*arrays, *waits))[: len(arrays)] if waits else arrays

    def run(names, step, state):
        state = tuple(after(names, state))
        if len(names) == 1:
            return step(names[0], *state)

        def steps(*state):
            for name in names:
                state = step(name, *state)
            return state

        return lax.cond(stretch_lengths[0] > 0, steps, lambda *state: state, *state)

    def runs(names):
        fences = [tuple(name for name in fence if name in names) for fence in FENCES]
        fences = [fence for fence in fences if fence]
        fenced = {name for fence in fences for name in fence}
        starts = {fence[0]: fence for fence in fences}
        return [starts.get(name, (name,)) for name in names if name in starts or name not in fenced]

    lane = np.arange(HD) % (HD // 2)
    frequency = jnp.asarray((ROPE_BASE ** (-2.0 * lane / HD)).astype(np.float32).reshape(1, HD))
    places = query_pos.reshape(query_count // HD, HD)
    parts = []
    for count, turn in CHUNKS:
        rotated = bits[turn:] + bits[:turn]
        first = bits[-turn]
        moved = (first,) + tuple(bit for bit in bits if bit != first)
        parts.append((rotated if turn >= 0 else moved, count))
    parts = tuple(parts)
    mass_steps = ["h.%d" % bit for bit in head_bits] + ["m.%d" % bit for bit in bits]
    mass_steps.sort(key=lambda name: MASS_ORDER.index(name) if name in MASS_ORDER else len(MASS_ORDER))
    orders = {}
    for order, _ in parts:
        orders.setdefault(order, len(orders))
    *halves, masses, raw_stats = flash(
        parts, group_size, queries, keys, values, stretch_lengths, places, frequency
    )
    keeps, sends = halves[: len(parts)], halves[len(parts) :]
    own = lax.optimization_barrier(in_log2(raw_stats))
    firsts = [order[0] for order in orders]

    def known(name):
        kind, bit = name.split(".")
        if kind == "h":
            return int(bit) in head_bits
        return int(bit) in bits

    stat_steps = ["a.%d" % bit for bit in bits]
    stat_runs, mass_runs = runs(stat_steps), runs(mass_steps[:-1]) + [(mass_steps[-1],)]
    run_of = {name: i for names in (stat_runs, mass_runs) for i, run_ in enumerate(names) for name in run_}

    @once
    def arrived(name):
        kind, bit = name.split(".")
        if kind == "a":
            return stats(run_of[name] + 1)[0]
        if kind in ("h", "m"):
            return mass(run_of[name] + 1)[0]
        n, bit = int(kind[1:]), int(bit)
        i = parts[n][0].index(bit)
        send = sends[n] if i == 0 else halved(n, i)[1]
        return exchange(after([name], (send,))[0], "ctx", bit)

    def stat_step(name, joined, *tops):
        bit = int(name.split(".")[1])
        opening = bit == bits[0]
        message = raw_stats if opening else joined
        if bit in firsts and not opening:
            message = jnp.concatenate([message, own[:STAT_ROWS]], axis=0)
        got = fenced(name, message, "ctx", bit)
        joined = join_stats(joined, in_log2(got) if opening else got[: 2 * STAT_ROWS])
        if bit in firsts:
            top = got[:STAT_ROWS] * LOG2_SCALE if opening else got[2 * STAT_ROWS :]
            tops = tuple(top if i == firsts.index(bit) else old for i, old in enumerate(tops))
        return (joined, *tops)

    def mass_step(name, total):
        kind, bit = name.split(".")
        return (total + fenced(name, total, "head" if kind == "h" else "ctx", int(bit)),)

    @once
    def stats(step):
        if step == 0:
            return (own,) + (own[:STAT_ROWS],) * len(firsts)
        return run(stat_runs[step - 1], stat_step, stats(step - 1))

    @once
    def weighed():
        joined, *tops = stats(len(stat_runs))
        factor = stretch_count / (heads_here * head_size)
        return weigh(tuple(orders), (heads_here,), stretch_count, factor, own, joined, tops, [masses])

    @once
    def mass(step):
        if step == 0:
            return (weighed()[0],)
        return run(mass_runs[step - 1], mass_step, mass(step - 1))

    @once
    def halved(n, i):
        order, count = parts[n]
        got = arrived("c%d.%d" % (n, order[i - 1]))
        if i == 1:
            first_head = sum(c for _, c in parts[:n])
            kind = orders[order]
            return merge(first_head, kind, keeps[n], got, weighed()[1 + kind])
        total = halved(n, i - 1)[0] + got
        rows = total.shape[0] // 2
        return total[:rows], total[rows:]

    last = len(bits) - 1
    totals = [halved(n, last)[0] for n in range(len(parts))]
    blocks = [arrived("c%d.%d" % (n, order[last])) for n, (order, _) in enumerate(parts)]
    name = mass_steps[-1]
    (before,) = mass(len(mass_runs) - 1)
    got = exchange(after([name], (before,))[0], "head" if name[0] == "h" else "ctx", int(name[2:]))
    return tuple(finish(totals, blocks, before, got))


def solution(mesh):
    placed = (P(None, "head"), P("ctx", "head"), P("ctx", "head"), P(), P())
    return jax.shard_map(
        local, mesh=mesh, in_specs=placed, out_specs=(P("ctx", "head"), P()), check_vma=False
    )
```
